128 devices in a mesh: scen: 8 (over z_hi, y), col: 16 (over x, z_lo, core).
Axes of the slice: x: 4, y: 4, z: 4 (z_hi: 2, z_lo: 2; z = z_hi * 2 + z_lo), core: 2. Of those that a mesh axis runs over, the one named last changes fastest.
Arguments:
- border: float32 [16, 2048, 16384], P('scen', None, 'col'), may hold values from -0.03314563 to 0.03314563
- pattern: int32 [16, 16, 128], P('scen', None, 'col'), may hold values 0 or 1
- slack: float32 [16, 2048], P('scen'), may hold values from 0.5 to 2
- first_diag: float32 [16384], P('col'), may hold values from 0.25 to 1.75
- rhs: float32 [16384, 256], P('col'), may hold values from -6 to 6
- scen_rhs: float32 [16, 2048, 256], P('scen', 'col'), may hold values from -6 to 6
Outputs:
- reduced: float32 [16, 1024, 256], P('col', 'scen')
- directions: float32 [16, 2048, 256], P('scen', 'col')
The draws below stay inside these ranges and needn't reach their ends.
All inputs are finite; a program needn't handle non-finite values. No bound on the sum of `pattern` on one device may be relied on, other than what follows from the above.
Results may differ from the reference program's by a relative error of at most 0.0001.
Values sent between devices are 32-bit elements; how exact they have to be, the bound alone decides.
No kernel may reach another device: no remote copies, remote signals or barrier semaphores. Data moves between devices by JAX's collectives and lax.ppermute only.
A program may use at most 128 MiB of HBM per device.

```python
import math
import jax
import jax.numpy as jnp
from jax import lax

N0 = 16384
PW = 512
NRHS = 256
ROWS = 2048
ROW_BLOCK = 128
COL_BLOCK = 128
SCEN_ALL = 16
FS_DEV = 1024
N_COL = 16


def draw_border(key, part):
    key_parts = jax.random.split(jax.random.fold_in(key, 7), 3)
    entry_scale = 1.0 / math.sqrt(SCEN_ALL * ROWS)
    separate = jax.random.normal(key_parts[0], (SCEN_ALL, ROWS, N0), jnp.float32)
    common_share = 0.2
    shared_rows = jax.random.normal(key_parts[1], (SCEN_ALL, ROWS, 1), jnp.float32)
    loading = jax.random.uniform(key_parts[2], (1, 1, N0), jnp.float32, 0.6, 1.4)
    mixture = math.sqrt(common_share) * shared_rows * loading + math.sqrt(1.0 - common_share) * separate
    limit_value = 5.9 * entry_scale
    return jnp.clip(entry_scale * mixture, -limit_value, limit_value).astype(jnp.float32)


def set_ends(entries, key, least, top_value):
    shape = entries.shape
    spot = [jax.random.randint(jax.random.fold_in(key, axis), (), 0, shape[axis]) for axis in range(len(shape))]
    entries = entries.at[tuple(spot)].set(least)
    longest = shape.index(max(shape))
    spot[longest] = (spot[longest] + 1) % shape[longest]
    return entries.at[tuple(spot)].set(top_value)


def steps_of(rng, extent, shards, low, largest):
    def one(position, blocks):
        draws = jax.random.uniform(jax.random.fold_in(jax.random.fold_in(rng, 6), position), (blocks,), jnp.float32, low / len(shards), largest / len(shards))
        return jnp.repeat(jnp.exp(draws), extent[position] // blocks).reshape((-1,) + (1,) * (len(extent) - position - 1))

    gain = one(*shards[0])
    for cut in shards[1:]:
        gain = gain * one(*cut)
    return gain


def gaussian(stream_key, extent, spread, reach, cuts=(), kind=jnp.bfloat16):
    array = jax.random.normal(stream_key, extent, jnp.float32) * spread
    if len(cuts) > 0:
        array = steps_of(stream_key, extent, cuts, -0.22, 0.18) * array
    return jnp.clip(array, min=-reach, max=reach).astype(kind)


def setup_inputs(seed: int = 0) -> dict:
    arg_keys = jax.random.split(jax.random.key(seed), 7)
    return {
        "border": draw_border(jax.random.fold_in(arg_keys[6], 71), 0),
        "pattern": set_ends((jax.random.randint(arg_keys[1], (SCEN_ALL, ROWS // ROW_BLOCK, N0 // COL_BLOCK), 0, 4) < 3).astype(jnp.int32), jax.random.fold_in(arg_keys[1], 1), 0, 1),
        "slack": jnp.clip(jnp.exp(math.log(2.0) - 1.3862944 * jax.random.uniform(arg_keys[2], (SCEN_ALL, ROWS), jnp.float32) ** steps_of(arg_keys[2], (SCEN_ALL, ROWS), ((0, 8),), -0.2, 0.2)), 0.5, 2.0),
        "first_diag": jnp.clip(1.0 + 0.15 * jax.random.normal(arg_keys[3], (N0,), jnp.float32), 0.25, 1.75),
        "rhs": gaussian(arg_keys[4], (N0, NRHS), 1.0, 6.0, ((0, 16),), jnp.float32),
        "scen_rhs": gaussian(arg_keys[5], (SCEN_ALL, ROWS, NRHS), 1.0, 6.0, ((0, 8), (1, 16)), jnp.float32),
    }


def expand(block_mask):
    ones = jnp.repeat(block_mask.astype(jnp.float32), ROW_BLOCK, axis=0)
    return jnp.repeat(ones, COL_BLOCK, axis=1)

def panel_index():
    order = jnp.arange(PW, dtype=jnp.int32)
    width_each = PW // N_COL
    return (order // width_each * (N0 // N_COL) + order % width_each).astype(jnp.int32)

def reference(border, pattern, slack, first_diag, rhs, scen_rhs):
    chosen = panel_index()
    order = jnp.arange(PW, dtype=jnp.int32)

    def accumulate(running, members):
        block_rows, block_mask, barrier = members
        masked = block_rows * expand(block_mask)
        panel_part = masked[:, chosen] / barrier[:, None]
        added = jnp.dot(masked.T.astype(jnp.float32), panel_part.astype(jnp.float32), precision=lax.Precision.HIGHEST, preferred_element_type=jnp.float32)
        return (running + added, None)
    schur, _ = lax.scan(accumulate, jnp.zeros((N0, PW), jnp.float32), (border, pattern, slack))
    schur = schur.at[chosen, order].add(first_diag[chosen])
    factor = jnp.linalg.cholesky(schur[chosen])
    forward = lax.linalg.triangular_solve(factor, rhs[chosen], left_side=True, lower=True)
    solved = lax.linalg.triangular_solve(factor, forward, left_side=True, lower=True, transpose_a=True)
    reduced = rhs - jnp.dot(schur.astype(jnp.float32), solved.astype(jnp.float32), precision=lax.Precision.HIGHEST, preferred_element_type=jnp.float32)
    reduced = reduced.at[chosen].set(forward)

    def direction(members):
        block_rows, block_mask, barrier, second_rhs = members
        panel_part = (block_rows * expand(block_mask))[:, chosen]
        moved = jnp.dot(panel_part.astype(jnp.float32), solved.astype(jnp.float32), precision=lax.Precision.HIGHEST, preferred_element_type=jnp.float32)
        return (second_rhs - moved) / barrier[:, None]
    directions = lax.map(direction, (border, pattern, slack, scen_rhs))
    return (reduced.reshape(N0 // FS_DEV, FS_DEV, NRHS), directions)
```

```python
import jax
import jax.numpy as jnp
from jax import lax
from jax.experimental import pallas as pl
from jax.experimental.pallas import tpu as pltpu
from jax.sharding import Mesh, PartitionSpec as P

PW = 512
BLOCK = 128
SLAB = 8
F32 = jnp.float32
BF16 = jnp.bfloat16
COL = ("chip", "core")
ALL_CHIPS = ("scen", "chip")
VMEM = pl.BlockSpec(memory_space=pltpu.VMEM)
PARAMS = pltpu.CompilerParams(vmem_limit_bytes=48 << 20)


def dot(a, b, dims, precision=lax.Precision.HIGHEST):
    return lax.dot_general(a, b, (dims, ((), ())), precision=precision, preferred_element_type=F32)


def dot_nn(a, b):
    return dot(a, b, ((1,), (0,)))


def dot_tn(a, b):
    return dot(a, b, ((0,), (0,)))


def dot_nt(a, b):
    return dot(a, b, ((1,), (1,)))


def panel_kernel(pattern, border, rhs, row_out, all_out):
    scen = pl.program_id(0)
    width = rhs.shape[0]
    blocks = row_out.shape[0]
    for i in range(blocks):
        rows = border[0, i * BLOCK : (i + 1) * BLOCK, :].T[:width]
        rows = rows * pattern[scen, i, 0].astype(F32)
        row_out[i, 0] = rows
        all_out[scen * blocks + i] = rows

    @pl.when(scen == 0)
    def _():
        for h in range(2):
            all_out[2 * blocks + h] = rhs[:, h * BLOCK : (h + 1) * BLOCK]


def pivot_kernel(core, mine, slack, diag, out):
    size = diag.shape[1]
    parts = [mine[:, s].reshape(size, BLOCK) for s in range(2)]
    right = jnp.concatenate(parts, axis=1)
    left = jnp.concatenate([parts[s] / slack[s : s + 1, :] for s in range(2)], axis=1)
    rows = lax.broadcasted_iota(jnp.int32, (size, BLOCK), 0)
    cols = lax.broadcasted_iota(jnp.int32, (size, BLOCK), 1)
    for q in range(4):
        piece = dot_nt(left, right[q * BLOCK : (q + 1) * BLOCK])
        piece = piece + jnp.where(rows == cols + q * BLOCK, diag[:, q * BLOCK : (q + 1) * BLOCK], 0.0)
        out[lax.rem(q + 2 * core[0], 4)] = piece


def schur_kernel(border, panel, slack, mask, out, left, right):
    step = pl.program_id(0)
    size = out.shape[1]
    count = panel.shape[1]
    depth = count * BLOCK
    for e in range(count):
        index = step * count + e
        piece = panel[:, e].reshape(size, BLOCK) / slack[pl.ds(index, 1), :]
        high = piece.astype(BF16)
        low = (piece - high.astype(F32)).astype(BF16)
        at = e * BLOCK
        left[:, at : at + BLOCK] = high
        left[:, depth + at : depth + at + BLOCK] = high
        left[:, 2 * depth + at : 2 * depth + at + BLOCK] = low
        rows = border[0, at : at + BLOCK, :] * mask[pl.ds(index, 1), :]
        high = rows.astype(BF16)
        low = (rows - high.astype(F32)).astype(BF16)
        right[at : at + BLOCK, :] = high
        right[depth + at : depth + at + BLOCK, :] = low
        right[2 * depth + at : 2 * depth + at + BLOCK, :] = high

    @pl.when(step == 0)
    def _():
        out[...] = jnp.zeros_like(out)

    wide = 2 * BLOCK
    for n in range(right.shape[1] // wide):
        piece = dot(left[...], right[:, n * wide : (n + 1) * wide], ((1,), (0,)), lax.Precision.DEFAULT)
        out[2 * n] += piece[:, :BLOCK]
        out[2 * n + 1] += piece[:, BLOCK:]


def eliminate(w):
    for first in range(0, BLOCK, SLAB):
        height = BLOCK - first
        cols = [jnp.broadcast_to(w[first:, first + k : first + k + 1], (height, BLOCK)) for k in range(SLAB)]
        left, right = w[first : first + SLAB, :BLOCK], w[first : first + SLAB, BLOCK:]
        lower, upper = [], []
        for k in range(SLAB):
            scale = lax.rsqrt(cols[k][k : k + 1, :])
            square = scale * scale
            for m in range(k + 1, SLAB):
                cols[m] = cols[m] - cols[k] * (cols[k][m : m + 1, :] * square)
            low = cols[k] * scale
            u0 = left[k : k + 1, :] * scale
            u1 = right[k : k + 1, :] * scale
            if k + 1 < SLAB:
                left = left - low[:SLAB] * u0
                right = right - low[:SLAB] * u1
            w[first + k : first + k + 1, BLOCK:] = u1
            lower.append(low)
            upper.append((u0, u1))
        if height > SLAB:
            rest0, rest1 = w[first + SLAB :, :BLOCK], w[first + SLAB :, BLOCK:]
            for k in range(SLAB):
                rest0 = rest0 - lower[k][SLAB:] * upper[k][0]
                rest1 = rest1 - lower[k][SLAB:] * upper[k][1]
            w[first + SLAB :, :BLOCK] = rest0
            w[first + SLAB :, BLOCK:] = rest1


def solve_kernel(core, mine, other, rhs, fwd, sol, m, w, linv):
    size, width = fwd.shape
    steps = size // BLOCK
    for q in range(2):
        here = pl.ds(pl.multiple_of((q + 2 * core[0]) * BLOCK, BLOCK), BLOCK)
        m[:, here] = mine[q]
        here = pl.ds(pl.multiple_of((q + 2 * (1 - core[0])) * BLOCK, BLOCK), BLOCK)
        m[:, here] = other[q]
        m[:, size + q * BLOCK : size + (q + 1) * BLOCK] = rhs[:, q].reshape(size, BLOCK)
    shape = (BLOCK, BLOCK)
    eye = (lax.broadcasted_iota(jnp.int32, shape, 0) == lax.broadcasted_iota(jnp.int32, shape, 1)).astype(F32)

    def outer(step, carry):
        here = pl.ds(pl.multiple_of(step * BLOCK, BLOCK), BLOCK)
        w[:, :BLOCK] = m[here, here]
        w[:, BLOCK:] = eye
        eliminate(w)
        inverse = w[:, BLOCK:]
        linv[step] = inverse
        m[here, :] = dot_nn(inverse, m[here, :])

        def update(later, inner):
            there = pl.ds(pl.multiple_of(later * BLOCK, BLOCK), BLOCK)
            m[there, :] = m[there, :] - dot_tn(m[here, there], m[here, :])
            return inner

        lax.fori_loop(step + 1, steps, update, 0)
        return carry

    lax.fori_loop(0, steps, outer, 0)
    fwd[...] = m[:, size:]
    for step in reversed(range(steps)):
        rows = slice(step * BLOCK, (step + 1) * BLOCK)
        total = m[rows, size:]
        if step + 1 < steps:
            after = (step + 1) * BLOCK
            total = total - dot_nn(m[rows, after:size], sol[after:, :])
        sol[rows, :] = dot_tn(linv[step], total)


def finish_kernel(place, schur, sol, fwd, rhs, mine, slack, scen_rhs, reduced, directions):
    size = sol.shape[0]
    width = size // mine.shape[0]
    total = schur[0]
    for k in range(1, schur.shape[0]):
        total = total + schur[k]
    solved = sol[...]
    result = rhs[...] - dot_tn(total, solved)
    reduced[0] = result

    @pl.when(place[0] == 0)
    def _():
        reduced[0, :width] = fwd[pl.ds(pl.multiple_of(place[1] * width, width), width), :]

    for s in range(2):
        moved = dot_tn(mine[:, s].reshape(size, BLOCK), solved)
        divisor = jnp.broadcast_to(slack[s : s + 1, :], (BLOCK, BLOCK)).T
        for h in range(moved.shape[1] // BLOCK):
            lanes = slice(h * BLOCK, (h + 1) * BLOCK)
            directions[s, :, lanes] = (scen_rhs[s, :, lanes] - moved[:, lanes]) / divisor


def per_device(border, pattern, slack, first_diag, rhs, scen_rhs):
    scen_index = lax.axis_index("scen")
    core_index = lax.axis_index("core")
    col_index = lax.axis_index("chip") * 2 + core_index
    cols = lax.axis_size("chip") * 2
    scens = lax.axis_size("scen")
    chips = lax.axis_size("chip") * scens
    own, row_total, own_width = border.shape
    width = PW // cols
    nrhs = rhs.shape[1]
    blocks = row_total // BLOCK
    smem = pl.BlockSpec(memory_space=pltpu.SMEM)

    row_blocks, all_blocks = pl.pallas_call(
        panel_kernel,
        grid=(own,),
        in_specs=[
            smem,
            pl.BlockSpec((1, row_total, BLOCK), lambda s: (s, 0, 0)),
            pl.BlockSpec((width, nrhs), lambda s: (0, 0)),
        ],
        out_specs=[
            pl.BlockSpec((blocks, 1, width, BLOCK), lambda s: (0, s, 0, 0)),
            pl.BlockSpec((own * blocks + 2, width, BLOCK), lambda s: (0, 0, 0)),
        ],
        out_shape=[
            jax.ShapeDtypeStruct((blocks, own, width, BLOCK), F32),
            jax.ShapeDtypeStruct((own * blocks + 2, width, BLOCK), F32),
        ],
        compiler_params=PARAMS,
        name="panel",
    )(pattern, border, rhs)

    mine = lax.all_to_all(row_blocks, COL, 0, 0, tiled=True)
    gathered = lax.all_gather(all_blocks, COL)

    slack_mine = lax.dynamic_slice_in_dim(slack, col_index * BLOCK, BLOCK, 1)
    diag = jnp.where(scen_index == 0, first_diag[:width], 0.0)
    diag = lax.dynamic_update_slice_in_dim(jnp.zeros((PW,), F32), diag, col_index * width, 0).reshape(1, PW)
    core = core_index.reshape(1).astype(jnp.int32)
    pivots = pl.pallas_call(
        pivot_kernel,
        in_specs=[smem, VMEM, VMEM, VMEM],
        out_specs=VMEM,
        out_shape=jax.ShapeDtypeStruct((4, PW, BLOCK), F32),
        compiler_params=PARAMS,
        name="pivot",
    )(core, mine, slack_mine, diag)

    swap = [(0, 1), (1, 0)]
    pair = pivots[:2] + lax.ppermute(pivots[2:], "core", swap)
    pair = lax.all_to_all(pair.reshape(chips, 2 * PW // chips, BLOCK), ALL_CHIPS, 0, 0, tiled=True)
    share = jnp.sum(pair, axis=0)
    share = lax.all_to_all(jnp.broadcast_to(share[None], pair.shape), ALL_CHIPS, 0, 0, tiled=True)
    half = share.reshape(2, PW, BLOCK)
    other = lax.ppermute(half, "core", swap)

    steps = 8
    count = own * blocks // steps
    mask = jnp.repeat(pattern.reshape(own * blocks, -1).astype(F32), BLOCK, axis=1)
    per_scen = blocks // count
    schur = pl.pallas_call(
        schur_kernel,
        grid=(steps,),
        in_specs=[
            pl.BlockSpec((1, count * BLOCK, own_width), lambda t: (t // per_scen, t % per_scen, 0)),
            pl.BlockSpec((cols, count, width, BLOCK), lambda t: (0, t, 0, 0)),
            pl.BlockSpec((own * blocks, BLOCK), lambda t: (0, 0)),
            pl.BlockSpec((own * blocks, own_width), lambda t: (0, 0)),
        ],
        out_specs=pl.BlockSpec((scens, PW, own_width // scens), lambda t: (0, 0, 0)),
        out_shape=jax.ShapeDtypeStruct((scens, PW, own_width // scens), F32),
        scratch_shapes=[
            pltpu.VMEM((PW, 3 * count * BLOCK), BF16),
            pltpu.VMEM((3 * count * BLOCK, own_width), BF16),
        ],
        compiler_params=PARAMS,
        cost_estimate=pl.CostEstimate(
            flops=6 * own * row_total * own_width * PW, bytes_accessed=28 << 20, transcendentals=0
        ),
        name="schur",
    )(border, gathered, slack.reshape(own * blocks, BLOCK), mask)
    schur = lax.all_to_all(schur, "scen", 0, 0, tiled=True)

    fwd, sol = pl.pallas_call(
        solve_kernel,
        grid=(1,),
        in_specs=[
            smem,
            pl.BlockSpec((2, PW, BLOCK), lambda t: (0, 0, 0)),
            pl.BlockSpec((2, PW, BLOCK), lambda t: (0, 0, 0)),
            pl.BlockSpec((cols, 2, width, BLOCK), lambda t: (0, own * blocks // 2, 0, 0)),
        ],
        out_specs=[pl.BlockSpec((PW, nrhs), lambda t: (0, 0))] * 2,
        out_shape=[jax.ShapeDtypeStruct((PW, nrhs), F32)] * 2,
        scratch_shapes=[
            pltpu.VMEM((PW, PW + nrhs), F32),
            pltpu.VMEM((BLOCK, 2 * BLOCK), F32),
            pltpu.VMEM((PW // BLOCK, BLOCK, BLOCK), F32),
        ],
        compiler_params=PARAMS,
        cost_estimate=pl.CostEstimate(flops=20 << 30, bytes_accessed=3 << 20, transcendentals=0),
        name="solve",
    )(core, half, other, gathered)

    place = jnp.stack([scen_index, col_index]).astype(jnp.int32)
    own_share = own_width // scens
    reduced, directions = pl.pallas_call(
        finish_kernel,
        grid_spec=pltpu.PrefetchScalarGridSpec(
            num_scalar_prefetch=1,
            grid=(1,),
            in_specs=[
                pl.BlockSpec((scens, PW, own_share), lambda t, place: (0, 0, 0)),
                pl.BlockSpec((PW, nrhs), lambda t, place: (0, 0)),
                pl.BlockSpec((PW, nrhs), lambda t, place: (0, 0)),
                pl.BlockSpec((own_share, nrhs), lambda t, place: (place[0], 0)),
                pl.BlockSpec((cols, own, width, BLOCK), lambda t, place: (0, 0, 0, 0)),
                pl.BlockSpec((own, BLOCK), lambda t, place: (0, 0)),
                pl.BlockSpec((own, BLOCK, nrhs), lambda t, place: (0, 0, 0)),
            ],
            out_specs=[
                pl.BlockSpec((1, own_share, nrhs), lambda t, place: (0, 0, 0)),
                pl.BlockSpec((own, BLOCK, nrhs), lambda t, place: (0, 0, 0)),
            ],
        ),
        out_shape=[
            jax.ShapeDtypeStruct((1, own_share, nrhs), F32),
            jax.ShapeDtypeStruct((own, BLOCK, nrhs), F32),
        ],
        compiler_params=PARAMS,
        name="finish",
    )(place, schur, sol, fwd, rhs, mine, slack_mine, scen_rhs)
    return reduced, directions


def solution(mesh):
    scens, cols = mesh.devices.shape
    split = Mesh(mesh.devices.reshape(scens, cols // 2, 2), ("scen", "chip", "core"))
    return jax.shard_map(
        per_device,
        mesh=split,
        in_specs=(
            P("scen", None, COL),
            P("scen", None, COL),
            P("scen", None),
            P(COL),
            P(COL, None),
            P("scen", COL, None),
        ),
        out_specs=(P(COL, "scen", None), P("scen", COL, None)),
        check_vma=False,
    )
```

```python
import jax
import jax.numpy as jnp
from jax import lax
from jax.experimental import pallas as pl
from jax.experimental.pallas import tpu as pltpu
from jax.sharding import Mesh, PartitionSpec as P

PW = 512
BLOCK = 128
SLAB = 8
STEPS = 8
F32 = jnp.float32
BF16 = jnp.bfloat16
COL = ("x", "z", "core")
SWAP = [(0, 1), (1, 0)]
ALL_CHIPS = ("scen", "x", "z")
DONE = jax.ShapeDtypeStruct((8, 128), F32)
DONE_SPEC = pl.BlockSpec((8, 128), lambda t: (0, 0))
ANY = pl.BlockSpec(memory_space=pl.ANY)
VMEM = pl.BlockSpec(memory_space=pltpu.VMEM)
LIMIT = 60 << 20
PARAMS = pltpu.CompilerParams(vmem_limit_bytes=LIMIT)


def dot(a, b, dims, precision=lax.Precision.HIGHEST):
    return lax.dot_general(a, b, (dims, ((), ())), precision=precision, preferred_element_type=F32)


def dot_nn(a, b):
    return dot(a, b, ((1,), (0,)))


def dot_tn(a, b):
    return dot(a, b, ((0,), (0,)))


def dot_nt(a, b):
    return dot(a, b, ((1,), (1,)))


def panel_kernel(pattern, border, rhs, row_out, all_out):
    scen = pl.program_id(0)
    width = rhs.shape[0]
    blocks = row_out.shape[0]
    for i in range(blocks):
        rows = border[0, i * BLOCK : (i + 1) * BLOCK, :].T[:width]
        rows = rows * pattern[scen, i, 0].astype(F32)
        row_out[i, 0] = rows
        all_out[scen * blocks + i] = rows

    @pl.when(scen == 0)
    def _():
        for h in range(2):
            all_out[2 * blocks + h] = rhs[:, h * BLOCK : (h + 1) * BLOCK]


def pivot_kernel(core, mine, slack, diag, *refs):
    kept, sent = refs[4], refs[5]
    size = diag.shape[1]
    parts = [mine[:, s].reshape(size, BLOCK) for s in range(2)]
    right = jnp.concatenate(parts, axis=1)
    left = jnp.concatenate([parts[s] / slack[s : s + 1, :] for s in range(2)], axis=1)
    rows = lax.broadcasted_iota(jnp.int32, (size, BLOCK), 0)
    cols = lax.broadcasted_iota(jnp.int32, (size, BLOCK), 1)
    for q in range(4):
        piece = dot_nt(left, right[q * BLOCK : (q + 1) * BLOCK])
        piece = piece + jnp.where(rows == cols + q * BLOCK, diag[:, q * BLOCK : (q + 1) * BLOCK], 0.0)

        @pl.when(core[0] == q // 2)
        def _():
            kept[q % 2] = piece

        @pl.when(core[0] != q // 2)
        def _():
            sent[q % 2] = piece


def total_kernel(pair, *refs):
    shared = refs[5]
    total = pair[0]
    for k in range(1, pair.shape[0]):
        total = total + pair[k]
    for k in range(pair.shape[0]):
        shared[k] = total


def split(values):
    high = values.astype(BF16)
    return high, (values - high.astype(F32)).astype(BF16)


def mask_kernel(pattern, border, _, out, done):
    step = pl.program_id(0)
    done[...] = jnp.zeros_like(done)
    depth, width = border.shape[1:]
    count = depth // BLOCK
    for e in range(count):
        index = step * count + e
        at = e * BLOCK
        for c in range(width // BLOCK):
            lanes = slice(c * BLOCK, (c + 1) * BLOCK)
            weight = pattern[index, c].astype(F32)
            high, low = split(border[0, at : at + BLOCK, lanes] * weight)
            out[0, at : at + BLOCK, lanes] = high
            out[0, depth + at : depth + at + BLOCK, lanes] = low


def mask_parts(pattern, border, after):
    scenarios, row_total, own_width = border.shape
    depth = scenarios * row_total // STEPS
    per_scen = row_total // depth
    return pl.pallas_call(
        mask_kernel,
        grid=(STEPS,),
        in_specs=[
            pl.BlockSpec(memory_space=pltpu.SMEM),
            pl.BlockSpec((1, depth, own_width), lambda t: (t // per_scen, t % per_scen, 0)),
            ANY,
        ],
        out_specs=[pl.BlockSpec((1, 2 * depth, own_width), lambda t: (t, 0, 0)), DONE_SPEC],
        out_shape=[jax.ShapeDtypeStruct((STEPS, 2 * depth, own_width), BF16), DONE],
        compiler_params=pltpu.CompilerParams(vmem_limit_bytes=LIMIT),
        cost_estimate=pl.CostEstimate(flops=0, bytes_accessed=40 << 20, transcendentals=0),
        name="mask",
    )(pattern, border, after)


def follow_kernel(*refs):
    del refs


def schur_kernel(*refs):
    masked, slack, _, _, *pieces, out, done, left = refs
    step = pl.program_id(0)
    done[...] = jnp.zeros_like(done)
    count, width = pieces[0].shape[:2]
    depth = count * BLOCK
    for e in range(count):
        inverse = 1.0 / slack[pl.ds(step * count + e, 1), :]
        at = e * BLOCK
        for k, piece in enumerate(pieces):
            high, low = split(piece[e] * inverse)
            rows = slice(k * width, (k + 1) * width)
            left[rows, at : at + BLOCK] = high
            left[rows, depth + at : depth + at + BLOCK] = high
            left[rows, 2 * depth + at : 2 * depth + at + BLOCK] = low

    @pl.when(step == 0)
    def _():
        out[...] = jnp.zeros_like(out)

    wide = 2 * BLOCK
    for n in range(masked.shape[2] // wide):
        lanes = slice(n * wide, (n + 1) * wide)
        dims = ((1,), (0,))
        product = dot(left[:, : 2 * depth], masked[0, :, lanes], dims, lax.Precision.DEFAULT)
        product += dot(left[:, 2 * depth :], masked[0, :depth, lanes], dims, lax.Precision.DEFAULT)
        out[2 * n] += product[:, :BLOCK]
        out[2 * n + 1] += product[:, BLOCK:]


def schur_product(masked, slack, pieces, scens, part, earlier, after):
    steps, depth, own_width = masked.shape
    depth //= 2
    width = pieces[0].shape[1]
    count = depth // BLOCK
    shape = (scens, len(pieces) * width, own_width // scens)
    whole = (scens, 2 * shape[1], shape[2])
    return pl.pallas_call(
        schur_kernel,
        grid=(steps,),
        in_specs=[
            pl.BlockSpec((1, 2 * depth, own_width), lambda t: (t, 0, 0)),
            pl.BlockSpec(slack.shape, lambda t: (0, 0)),
            ANY,
            ANY,
        ]
        + [pl.BlockSpec((count, width, BLOCK), lambda t: (t, 0, 0))] * len(pieces),
        out_specs=[pl.BlockSpec(shape, lambda t: (0, part, 0)), DONE_SPEC],
        out_shape=[jax.ShapeDtypeStruct(whole, F32), DONE],
        input_output_aliases={2: 0} if part else {},
        scratch_shapes=[pltpu.VMEM((shape[1], 3 * depth), BF16)],
        compiler_params=pltpu.CompilerParams(vmem_limit_bytes=LIMIT),
        cost_estimate=pl.CostEstimate(
            flops=6 * steps * depth * own_width * shape[1], bytes_accessed=20 << 20, transcendentals=0
        ),
        name="schur",
    )(masked, slack, earlier, after, *pieces)


def eliminate(w):
    for first in range(0, BLOCK, SLAB):
        height = BLOCK - first
        cols = [jnp.broadcast_to(w[first:, first + k : first + k + 1], (height, BLOCK)) for k in range(SLAB)]
        left, right = w[first : first + SLAB, :BLOCK], w[first : first + SLAB, BLOCK:]
        lower, upper = [], []
        for k in range(SLAB):
            scale = lax.rsqrt(cols[k][k : k + 1, :])
            square = scale * scale
            for m in range(k + 1, SLAB):
                cols[m] = cols[m] - cols[k] * (cols[k][m : m + 1, :] * square)
            low = cols[k] * scale
            u0 = left[k : k + 1, :] * scale
            u1 = right[k : k + 1, :] * scale
            if k + 1 < SLAB:
                left = left - low[:SLAB] * u0
                right = right - low[:SLAB] * u1
            w[first + k : first + k + 1, BLOCK:] = u1
            lower.append(low)
            upper.append((u0, u1))
        if height > SLAB:
            rest0, rest1 = w[first + SLAB :, :BLOCK], w[first + SLAB :, BLOCK:]
            for k in range(SLAB):
                rest0 = rest0 - lower[k][SLAB:] * upper[k][0]
                rest1 = rest1 - lower[k][SLAB:] * upper[k][1]
            w[first + SLAB :, :BLOCK] = rest0
            w[first + SLAB :, BLOCK:] = rest1


def row_of(order, core, k, width):
    place = core[0] if k % 2 == 0 else 1 - core[0]
    return pl.multiple_of((2 * order[k // 2] + place) * width, width)


def solve_kernel(core, order, mine, other, *refs):
    *pieces, _, fwd, sol, m, w, linv = refs
    size = fwd.shape[0]
    steps = size // BLOCK
    width = pieces[0].shape[1]
    for q in range(2):
        here = pl.ds(pl.multiple_of((q + 2 * core[0]) * BLOCK, BLOCK), BLOCK)
        m[:, here] = mine[q]
        here = pl.ds(pl.multiple_of((q + 2 * (1 - core[0])) * BLOCK, BLOCK), BLOCK)
        m[:, here] = other[q]
        for k, piece in enumerate(pieces):
            m[pl.ds(row_of(order, core, k, width), width), size + q * BLOCK : size + (q + 1) * BLOCK] = piece[q]
    shape = (BLOCK, BLOCK)
    eye = (lax.broadcasted_iota(jnp.int32, shape, 0) == lax.broadcasted_iota(jnp.int32, shape, 1)).astype(F32)

    def outer(step, carry):
        here = pl.ds(pl.multiple_of(step * BLOCK, BLOCK), BLOCK)
        w[:, :BLOCK] = m[here, here]
        w[:, BLOCK:] = eye
        eliminate(w)
        inverse = w[:, BLOCK:]
        linv[step] = inverse
        m[here, :] = dot_nn(inverse, m[here, :])

        def update(later, inner):
            there = pl.ds(pl.multiple_of(later * BLOCK, BLOCK), BLOCK)
            m[there, :] = m[there, :] - dot_tn(m[here, there], m[here, :])
            return inner

        lax.fori_loop(step + 1, steps, update, 0)
        return carry

    lax.fori_loop(0, steps, outer, 0)
    fwd[...] = m[:, size:]
    for step in reversed(range(steps)):
        rows = slice(step * BLOCK, (step + 1) * BLOCK)
        total = m[rows, size:]
        if step + 1 < steps:
            after = (step + 1) * BLOCK
            total = total - dot_nn(m[rows, after:size], sol[after:, :])
        sol[rows, :] = dot_tn(linv[step], total)


def finish_kernel(place, core, order, schur, sol, fwd, rhs, mine, slack, scen_rhs, reduced, directions, moved_sol):
    size = sol.shape[0]
    width = size // mine.shape[0]
    for k in range(mine.shape[0]):
        moved_sol[k * width : (k + 1) * width, :] = sol[pl.ds(row_of(order, core, k, width), width), :]
    solved = sol[...]
    total = schur[0]
    for k in range(1, schur.shape[0]):
        total = total + schur[k]
    result = rhs[...] - dot_tn(total, moved_sol[...])
    reduced[0] = result

    @pl.when(place[0] == 0)
    def _():
        reduced[0, :width] = fwd[pl.ds(pl.multiple_of(place[1] * width, width), width), :]

    for s in range(2):
        moved = dot_tn(mine[:, s].reshape(size, BLOCK), solved)
        divisor = jnp.broadcast_to(slack[s : s + 1, :], (BLOCK, BLOCK)).T
        for h in range(moved.shape[1] // BLOCK):
            lanes = slice(h * BLOCK, (h + 1) * BLOCK)
            directions[s, :, lanes] = (scen_rhs[s, :, lanes] - moved[:, lanes]) / divisor


def shape_of(value):
    return jax.ShapeDtypeStruct(value.shape, value.dtype)


def with_other_core(pieces):
    return [value for piece in pieces for value in (piece, lax.ppermute(piece, "core", SWAP))]


def per_device(border, pattern, slack, first_diag, rhs, scen_rhs):
    scen_index = lax.axis_index("scen")
    core_index = lax.axis_index("core")
    col_index = lax.axis_index(COL)
    cols = lax.axis_size(COL)
    scens = lax.axis_size("scen")
    chips = lax.axis_size(ALL_CHIPS)
    own, row_total, own_width = border.shape
    width = PW // cols
    nrhs = rhs.shape[1]
    blocks = row_total // BLOCK
    smem = pl.BlockSpec(memory_space=pltpu.SMEM)

    row_blocks, piece = pl.pallas_call(
        panel_kernel,
        grid=(own,),
        in_specs=[
            smem,
            pl.BlockSpec((1, row_total, BLOCK), lambda s: (s, 0, 0)),
            pl.BlockSpec((width, nrhs), lambda s: (0, 0)),
        ],
        out_specs=[
            pl.BlockSpec((blocks, 1, width, BLOCK), lambda s: (0, s, 0, 0)),
            pl.BlockSpec((own * blocks + 2, width, BLOCK), lambda s: (0, 0, 0)),
        ],
        out_shape=[
            jax.ShapeDtypeStruct((blocks, own, width, BLOCK), F32),
            jax.ShapeDtypeStruct((own * blocks + 2, width, BLOCK), F32),
        ],
        compiler_params=pltpu.CompilerParams(vmem_limit_bytes=LIMIT),
        name="panel",
    )(pattern, border, rhs)

    mine = lax.all_to_all(row_blocks, COL, 0, 0, tiled=True)
    along = lax.axis_size("x")
    up = [(a, (a + 1) % along) for a in range(along)]
    down = [(a, (a - 1) % along) for a in range(along)]
    below = lax.ppermute(piece, "x", up)
    above = lax.ppermute(piece, "x", down)
    beside = lax.ppermute(piece, "z", SWAP)
    masked, masked_done = mask_parts(pattern.reshape(own * blocks, -1), border, row_blocks)

    slack_mine = lax.dynamic_slice_in_dim(slack, col_index * BLOCK, BLOCK, 1)
    diag = jnp.where(scen_index == 0, first_diag[:width], 0.0)
    diag = lax.dynamic_update_slice_in_dim(jnp.zeros((PW,), F32), diag, col_index * width, 0).reshape(1, PW)
    core = core_index.reshape(1).astype(jnp.int32)
    half_shape = jax.ShapeDtypeStruct((2, PW, BLOCK), F32)
    kept, sent, below, above, beside = pl.pallas_call(
        pivot_kernel,
        in_specs=[smem, VMEM, VMEM, VMEM, ANY, ANY, ANY, ANY],
        out_specs=[VMEM, VMEM, ANY, ANY, ANY],
        out_shape=[half_shape, half_shape] + [shape_of(below)] * 3,
        input_output_aliases={5: 2, 6: 3, 7: 4},
        compiler_params=PARAMS,
        name="pivot",
    )(core, mine, slack_mine, diag, masked_done, below, above, beside)

    pair = kept + lax.ppermute(sent, "core", SWAP)
    pair = lax.all_to_all(pair.reshape(chips, 2 * PW // chips, BLOCK), ALL_CHIPS, 0, 0, tiled=True)
    middle = piece.shape[0] // 2
    far_up = lax.ppermute(below[:middle], "x", up)
    far_down = lax.ppermute(above[middle:], "x", down)
    below_beside = lax.ppermute(beside, "x", up)
    above_beside = lax.ppermute(beside, "x", down)
    slack_rows = slack.reshape(own * blocks, BLOCK)
    near_pieces = with_other_core([piece, below, above, beside])
    schur, near_done = schur_product(masked, slack_rows, near_pieces, scens, 0, masked_done, masked_done)

    share, far_up, far_down, below_beside, above_beside = pl.pallas_call(
        total_kernel,
        in_specs=[VMEM] + [ANY] * 5,
        out_specs=[VMEM] + [ANY] * 4,
        out_shape=[shape_of(v) for v in (pair, far_up, far_down, below_beside, above_beside)],
        input_output_aliases={2: 1, 3: 2, 4: 3, 5: 4},
        compiler_params=PARAMS,
        name="total",
    )(pair, near_done, far_up, far_down, below_beside, above_beside)
    half = lax.all_to_all(share, ALL_CHIPS, 0, 0, tiled=True).reshape(2, PW, BLOCK)
    other = lax.ppermute(half, "core", SWAP)
    opposite = jnp.concatenate([far_up, far_down])
    opposite_beside = lax.ppermute(opposite, "z", SWAP)
    opposite_beside = pl.pallas_call(
        follow_kernel,
        in_specs=[ANY, ANY],
        out_specs=ANY,
        out_shape=shape_of(opposite_beside),
        input_output_aliases={1: 0},
        compiler_params=PARAMS,
        name="follow",
    )(half, opposite_beside)
    far_pieces = with_other_core([below_beside, above_beside, opposite, opposite_beside])
    schur, far_done = schur_product(masked, slack_rows, far_pieces, scens, 1, schur, half)

    x, z = lax.axis_index("x"), lax.axis_index("z")
    steps = [(along - 1, z), (1, z), (along - 1, 1 - z), (1, 1 - z), (2, z), (2, 1 - z)]
    order = [x * 2 + z] + [lax.rem(x + step, along) * 2 + side for step, side in steps[:2]] + [x * 2 + 1 - z]
    order += [lax.rem(x + step, along) * 2 + side for step, side in steps[2:]]
    order = jnp.stack(order).astype(jnp.int32)
    pieces = near_pieces + far_pieces
    fwd, sol = pl.pallas_call(
        solve_kernel,
        grid=(1,),
        in_specs=[
            smem,
            smem,
            pl.BlockSpec((2, PW, BLOCK), lambda t: (0, 0, 0)),
            pl.BlockSpec((2, PW, BLOCK), lambda t: (0, 0, 0)),
        ]
        + [pl.BlockSpec((2, width, BLOCK), lambda t: (own * blocks // 2, 0, 0))] * len(pieces)
        + [ANY],
        out_specs=[pl.BlockSpec((PW, nrhs), lambda t: (0, 0))] * 2,
        out_shape=[jax.ShapeDtypeStruct((PW, nrhs), F32)] * 2,
        scratch_shapes=[
            pltpu.VMEM((PW, PW + nrhs), F32),
            pltpu.VMEM((BLOCK, 2 * BLOCK), F32),
            pltpu.VMEM((PW // BLOCK, BLOCK, BLOCK), F32),
        ],
        compiler_params=PARAMS,
        cost_estimate=pl.CostEstimate(flops=20 << 30, bytes_accessed=3 << 20, transcendentals=0),
        name="solve",
    )(core, order, half, other, *pieces, far_done)
    schur = lax.all_to_all(schur, "scen", 0, 0, tiled=True)

    place = jnp.stack([scen_index, col_index]).astype(jnp.int32)
    own_share = own_width // scens
    reduced, directions = pl.pallas_call(
        finish_kernel,
        grid_spec=pltpu.PrefetchScalarGridSpec(
            num_scalar_prefetch=3,
            grid=(1,),
            in_specs=[
                pl.BlockSpec(schur.shape, lambda t, *_: (0, 0, 0)),
                pl.BlockSpec((PW, nrhs), lambda t, *_: (0, 0)),
                pl.BlockSpec((PW, nrhs), lambda t, *_: (0, 0)),
                pl.BlockSpec((own_share, nrhs), lambda t, place, *_: (place[0], 0)),
                pl.BlockSpec((cols, own, width, BLOCK), lambda t, *_: (0, 0, 0, 0)),
                pl.BlockSpec((own, BLOCK), lambda t, *_: (0, 0)),
                pl.BlockSpec((own, BLOCK, nrhs), lambda t, *_: (0, 0, 0)),
            ],
            out_specs=[
                pl.BlockSpec((1, own_share, nrhs), lambda t, *_: (0, 0, 0)),
                pl.BlockSpec((own, BLOCK, nrhs), lambda t, *_: (0, 0, 0)),
            ],
            scratch_shapes=[pltpu.VMEM((PW, nrhs), F32)],
        ),
        out_shape=[
            jax.ShapeDtypeStruct((1, own_share, nrhs), F32),
            jax.ShapeDtypeStruct((own, BLOCK, nrhs), F32),
        ],
        compiler_params=PARAMS,
        name="finish",
    )(place, core, order, schur, sol, fwd, rhs, mine, slack_mine, scen_rhs)
    return reduced, directions


def solution(mesh):
    scens, cols = mesh.devices.shape
    parts = Mesh(mesh.devices.reshape(scens, cols // 4, 2, 2), ("scen", "x", "z", "core"))
    return jax.shard_map(
        per_device,
        mesh=parts,
        in_specs=(
            P("scen", None, COL),
            P("scen", None, COL),
            P("scen", None),
            P(COL),
            P(COL, None),
            P("scen", COL, None),
        ),
        out_specs=(P(COL, "scen", None), P("scen", COL, None)),
        check_vma=False,
    )
```

```python
import functools

import jax
import jax.numpy as jnp
from jax import lax
from jax.experimental import pallas as pl
from jax.experimental.pallas import tpu as pltpu
from jax.sharding import Mesh, PartitionSpec as P

PW = 512
BLOCK = 128
SLAB = 8
STEPS = 8
F32 = jnp.float32
BF16 = jnp.bfloat16
COL = ("x", "z", "core")
SWAP = [(0, 1), (1, 0)]
ALL_CHIPS = ("scen", "x", "z")
DONE = jax.ShapeDtypeStruct((8, 128), F32)
DONE_SPEC = pl.BlockSpec((8, 128), lambda t: (0, 0))
ANY = pl.BlockSpec(memory_space=pl.ANY)
VMEM = pl.BlockSpec(memory_space=pltpu.VMEM)
PARAMS = pltpu.CompilerParams(vmem_limit_bytes=20 << 20)
SHORT = pl.CostEstimate(flops=1 << 20, bytes_accessed=1 << 16, transcendentals=0)
WIDE_PARAMS = pltpu.CompilerParams(vmem_limit_bytes=56 << 20)


def dot(a, b, dims, precision=lax.Precision.HIGHEST):
    return lax.dot_general(a, b, (dims, ((), ())), precision=precision, preferred_element_type=F32)


def dot_nn(a, b):
    return dot(a, b, ((1,), (0,)))


def dot_tn(a, b):
    return dot(a, b, ((0,), (0,)))


def dot_nt(a, b):
    return dot(a, b, ((1,), (1,)))


def panel_kernel(pattern, border, rhs, row_out, all_out):
    scen = pl.program_id(0)
    width = rhs.shape[0]
    blocks = row_out.shape[0]
    for i in range(blocks):
        rows = border[0, i * BLOCK : (i + 1) * BLOCK, :].T[:width]
        rows = rows * pattern[scen, 0, i].astype(F32)
        row_out[i, 0] = rows
        all_out[scen * blocks + i] = rows

    @pl.when(scen == 0)
    def _():
        for h in range(2):
            all_out[2 * blocks + h] = rhs[:, h * BLOCK : (h + 1) * BLOCK]


def pivot_kernel(core, mine, slack, diag, *refs):
    kept, sent, right = refs[3], refs[4], refs[-1]
    size = diag.shape[1]
    for s in range(2):
        right[:, s * BLOCK : (s + 1) * BLOCK] = mine[:, s].reshape(size, BLOCK)
    left = jnp.concatenate([right[:, s * BLOCK : (s + 1) * BLOCK] / slack[s : s + 1, :] for s in range(2)], axis=1)
    rows = lax.broadcasted_iota(jnp.int32, (size, BLOCK), 0)
    cols = lax.broadcasted_iota(jnp.int32, (size, BLOCK), 1)
    for out, place in ((kept, core[0]), (sent, 1 - core[0])):
        for q in range(2):
            first = pl.multiple_of((q + 2 * place) * BLOCK, BLOCK)
            piece = dot_nt(left, right[pl.ds(first, BLOCK), :])
            out[q] = piece + jnp.where(rows == cols + first, diag[:, pl.ds(first, BLOCK)], 0.0)


def total_kernel(pair, *refs):
    shared = refs[4]
    total = pair[0]
    for k in range(1, pair.shape[0]):
        total = total + pair[k]
    for k in range(pair.shape[0]):
        shared[k] = total


def split(values):
    high = values.astype(BF16)
    return high, (values - high.astype(F32)).astype(BF16)


def mask_kernel(half, pattern, border, _, out, done):
    step = pl.program_id(0)
    done[...] = jnp.zeros_like(done)
    depth = border.shape[1]
    chunks, _, _, wide = out.shape
    per_scen = STEPS // pattern.shape[0]
    for e in range(depth // BLOCK):
        rows = slice(e * BLOCK, (e + 1) * BLOCK)
        block = lax.rem(step, per_scen) * (depth // BLOCK) + e
        for n in range(chunks):
            for c in range(wide // BLOCK):
                col = n * (wide // BLOCK) + c
                weight = pattern[lax.div(step, per_scen), half * chunks * (wide // BLOCK) + col, block].astype(F32)
                high, low = split(border[0, rows, col * BLOCK : (col + 1) * BLOCK] * weight)
                lanes = slice(c * BLOCK, (c + 1) * BLOCK)
                out[n, 0, rows, lanes] = high
                out[n, 1, rows, lanes] = low


def mask_parts(half, pattern, border, after):
    scenarios, row_total, own_width = border.shape
    rows = scenarios * row_total
    depth = rows // STEPS
    per_scen = row_total // depth
    wide = 2 * BLOCK
    chunks = own_width // 2 // wide
    return pl.pallas_call(
        functools.partial(mask_kernel, half),
        grid=(STEPS,),
        in_specs=[
            pl.BlockSpec(memory_space=pltpu.SMEM),
            pl.BlockSpec((1, depth, own_width // 2), lambda t: (t // per_scen, t % per_scen, half)),
            ANY,
        ],
        out_specs=[pl.BlockSpec((chunks, 2, depth, wide), lambda t: (0, 0, t, 0)), DONE_SPEC],
        out_shape=[jax.ShapeDtypeStruct((chunks, 2, rows, wide), BF16), DONE],
        compiler_params=WIDE_PARAMS,
        cost_estimate=SHORT,
        name="mask",
    )(pattern, border, after)


def follow_kernel(*refs):
    del refs


def follow(first, value):
    return pl.pallas_call(
        follow_kernel,
        in_specs=[ANY, ANY],
        out_specs=ANY,
        out_shape=shape_of(value),
        input_output_aliases={1: 0},
        compiler_params=PARAMS,
        cost_estimate=SHORT,
        name="follow",
    )(first, value)


def schur_kernel(part, masked_left, masked_right, slack, earlier, *refs):
    count = len(refs) - 10
    pieces, out, done = refs[:count], refs[count], refs[count + 1]
    high, low, held, right, result, sems, right_sems, out_sem = refs[count + 2 :]
    done[...] = jnp.zeros_like(done)
    blocks, width = held.shape[1:3]
    sources = [half.at[n] for half in (masked_left, masked_right) for n in range(half.shape[0])]
    loads = [
        pltpu.make_async_copy(source, right.at[n % 2], right_sems.at[n % 2]) for n, source in enumerate(sources)
    ]
    copies = [
        pltpu.make_async_copy(piece.at[pl.ds(0, blocks)], held.at[k], sems.at[k]) for k, piece in enumerate(pieces)
    ]
    for copy in copies:
        copy.start()
    loads[0].start()
    for k, copy in enumerate(copies):
        copy.wait()

        def prepare(e, carry):
            inverse = 1.0 / slack[pl.ds(e, 1), :]
            lanes = pl.ds(pl.multiple_of(e * BLOCK, BLOCK), BLOCK)
            rows = slice(k * width, (k + 1) * width)
            high[rows, lanes], low[rows, lanes] = split(held[k, e] * inverse)
            return carry

        lax.fori_loop(0, blocks, prepare, 0, unroll=4)
    dims = ((1,), (0,))
    for n, load in enumerate(loads):
        if n + 1 < len(loads):
            loads[n + 1].start()
        load.wait()
        product = dot(high[...], right[n % 2, 0], dims, lax.Precision.DEFAULT)
        product += dot(high[...], right[n % 2, 1], dims, lax.Precision.DEFAULT)
        product += dot(low[...], right[n % 2, 0], dims, lax.Precision.DEFAULT)
        result[2 * n] = product[:, :BLOCK]
        result[2 * n + 1] = product[:, BLOCK:]
    rows = result.shape[1]
    copy = pltpu.make_async_copy(result, out.at[:, pl.ds(part * rows, rows)], out_sem)
    copy.start()
    copy.wait()


def schur_product(masked, slack, pieces, scens, part, earlier):
    chunks, _, depth, wide = masked[0].shape
    own_width = 2 * chunks * wide
    width = pieces[0].shape[1]
    rows = len(pieces) * width
    whole = (scens, 2 * rows, own_width // scens)
    return pl.pallas_call(
        functools.partial(schur_kernel, part),
        in_specs=[ANY, ANY, VMEM, ANY] + [ANY] * len(pieces),
        out_specs=[ANY, VMEM],
        out_shape=[jax.ShapeDtypeStruct(whole, F32), DONE],
        input_output_aliases={3: 0} if part else {},
        scratch_shapes=[
            pltpu.VMEM((rows, depth), BF16),
            pltpu.VMEM((rows, depth), BF16),
            pltpu.VMEM((len(pieces), depth // BLOCK, width, BLOCK), F32),
            pltpu.VMEM((2, 2, depth, wide), BF16),
            pltpu.VMEM((scens, rows, own_width // scens), F32),
            pltpu.SemaphoreType.DMA((len(pieces),)),
            pltpu.SemaphoreType.DMA((2,)),
            pltpu.SemaphoreType.DMA,
        ],
        compiler_params=WIDE_PARAMS,
        cost_estimate=SHORT,
        name="schur",
    )(*masked, slack, earlier, *pieces)


def eliminate(w):
    for first in range(0, BLOCK, SLAB):
        height = BLOCK - first
        cols = [jnp.broadcast_to(w[first:, first + k : first + k + 1], (height, BLOCK)) for k in range(SLAB)]
        left, right = w[first : first + SLAB, :BLOCK], w[first : first + SLAB, BLOCK:]
        lower, upper = [], []
        for k in range(SLAB):
            scale = lax.rsqrt(cols[k][k : k + 1, :])
            square = scale * scale
            for m in range(k + 1, SLAB):
                cols[m] = cols[m] - cols[k] * (cols[k][m : m + 1, :] * square)
            low = cols[k] * scale
            u0 = left[k : k + 1, :] * scale
            u1 = right[k : k + 1, :] * scale
            if k + 1 < SLAB:
                left = left - low[:SLAB] * u0
                right = right - low[:SLAB] * u1
            w[first + k : first + k + 1, BLOCK:] = u1
            lower.append(low)
            upper.append((u0, u1))
        if height > SLAB:
            rest0, rest1 = w[first + SLAB :, :BLOCK], w[first + SLAB :, BLOCK:]
            for k in range(SLAB):
                rest0 = rest0 - lower[k][SLAB:] * upper[k][0]
                rest1 = rest1 - lower[k][SLAB:] * upper[k][1]
            w[first + SLAB :, :BLOCK] = rest0
            w[first + SLAB :, BLOCK:] = rest1


def rows_of(order, k, width):
    return pl.ds(pl.multiple_of(order[k] * width, width), width)


def solve_kernel(core, order, mine, other, *refs):
    *pieces, _, fwd, sol, m, w, linv = refs
    size = fwd.shape[0]
    steps = size // BLOCK
    width = pieces[0].shape[1]
    for q in range(2):
        here = pl.ds(pl.multiple_of((q + 2 * core[0]) * BLOCK, BLOCK), BLOCK)
        m[:, here] = mine[q]
        here = pl.ds(pl.multiple_of((q + 2 * (1 - core[0])) * BLOCK, BLOCK), BLOCK)
        m[:, here] = other[q]
        for k, piece in enumerate(pieces):
            m[rows_of(order, k, width), size + q * BLOCK : size + (q + 1) * BLOCK] = piece[q]
    shape = (BLOCK, BLOCK)
    eye = (lax.broadcasted_iota(jnp.int32, shape, 0) == lax.broadcasted_iota(jnp.int32, shape, 1)).astype(F32)

    def outer(step, carry):
        here = pl.ds(pl.multiple_of(step * BLOCK, BLOCK), BLOCK)
        w[:, :BLOCK] = m[here, here]
        w[:, BLOCK:] = eye
        eliminate(w)
        inverse = w[:, BLOCK:]
        linv[step] = inverse
        m[here, :] = dot_nn(inverse, m[here, :])

        def update(later, inner):
            there = pl.ds(pl.multiple_of(later * BLOCK, BLOCK), BLOCK)
            m[there, :] = m[there, :] - dot_tn(m[here, there], m[here, :])
            return inner

        lax.fori_loop(step + 1, steps, update, 0)
        return carry

    lax.fori_loop(0, steps, outer, 0)
    fwd[...] = m[:, size:]
    for step in reversed(range(steps)):
        rows = slice(step * BLOCK, (step + 1) * BLOCK)
        total = m[rows, size:]
        if step + 1 < steps:
            after = (step + 1) * BLOCK
            total = total - dot_nn(m[rows, after:size], sol[after:, :])
        sol[rows, :] = dot_tn(linv[step], total)


def directions_kernel(sol, mine, slack, scen_rhs, directions):
    size = sol.shape[0]
    solved = sol[...]
    for s in range(2):
        moved = dot_tn(mine[:, s].reshape(size, BLOCK), solved)
        divisor = jnp.broadcast_to(slack[s : s + 1, :], (BLOCK, BLOCK)).T
        for h in range(moved.shape[1] // BLOCK):
            lanes = slice(h * BLOCK, (h + 1) * BLOCK)
            directions[s, :, lanes] = (scen_rhs[s, :, lanes] - moved[:, lanes]) / divisor


def reduced_kernel(place, order, schur, sol, fwd, rhs, reduced, moved_sol):
    pieces = order.shape[0]
    width = sol.shape[0] // pieces
    for k in range(pieces):
        moved_sol[k * width : (k + 1) * width, :] = sol[rows_of(order, k, width), :]
    total = schur[0]
    for k in range(1, schur.shape[0]):
        total = total + schur[k]
    reduced[0] = rhs[...] - dot_tn(total, moved_sol[...])

    @pl.when(place[0] == 0)
    def _():
        reduced[0, :width] = fwd[rows_of(place, 1, width), :]


def shape_of(value):
    return jax.ShapeDtypeStruct(value.shape, value.dtype)


def with_other_core(pieces):
    return [value for piece in pieces for value in (piece, lax.ppermute(piece, "core", SWAP))]


def per_device(border, pattern, slack, first_diag, rhs, scen_rhs):
    scen_index = lax.axis_index("scen")
    core_index = lax.axis_index("core")
    pattern = jnp.transpose(pattern, (0, 2, 1))
    col_index = lax.axis_index(COL)
    cols = lax.axis_size(COL)
    scens = lax.axis_size("scen")
    chips = lax.axis_size(ALL_CHIPS)
    own, row_total, own_width = border.shape
    width = PW // cols
    nrhs = rhs.shape[1]
    blocks = row_total // BLOCK
    smem = pl.BlockSpec(memory_space=pltpu.SMEM)

    row_blocks, piece = pl.pallas_call(
        panel_kernel,
        grid=(own,),
        in_specs=[
            smem,
            pl.BlockSpec((1, row_total, BLOCK), lambda s: (s, 0, 0)),
            pl.BlockSpec((width, nrhs), lambda s: (0, 0)),
        ],
        out_specs=[
            pl.BlockSpec((blocks, 1, width, BLOCK), lambda s: (0, s, 0, 0)),
            pl.BlockSpec((own * blocks + 2, width, BLOCK), lambda s: (0, 0, 0)),
        ],
        out_shape=[
            jax.ShapeDtypeStruct((blocks, own, width, BLOCK), F32),
            jax.ShapeDtypeStruct((own * blocks + 2, width, BLOCK), F32),
        ],
        compiler_params=WIDE_PARAMS,
        name="panel",
    )(pattern, border, rhs)

    mine = lax.all_to_all(row_blocks, COL, 0, 0, tiled=True)
    along = lax.axis_size("x")
    first_way = [(2 * a + c, 2 * ((a + 1 - 2 * c) % along) + c) for a in range(along) for c in range(2)]
    second_way = [(target, source) for source, target in first_way]
    first = lax.ppermute(piece, ("x", "core"), first_way)
    second = lax.ppermute(piece, ("x", "core"), second_way)
    beside = lax.ppermute(piece, "z", SWAP)
    masked_left, masked_done = mask_parts(0, pattern, border, row_blocks)
    masked_right, masked_done = mask_parts(1, pattern, border, masked_done)
    masked = (masked_left, masked_right)
    first = follow(masked_done, first)
    opposite = lax.ppermute(first, ("x", "core"), first_way)

    slack_mine = lax.dynamic_slice_in_dim(slack, col_index * BLOCK, BLOCK, 1)
    diag = jnp.where(scen_index == 0, first_diag[:width], 0.0)
    diag = lax.dynamic_update_slice_in_dim(jnp.zeros((PW,), F32), diag, col_index * width, 0).reshape(1, PW)
    core = core_index.reshape(1).astype(jnp.int32)
    half_shape = jax.ShapeDtypeStruct((2, PW, BLOCK), F32)
    kept, sent, second, beside = pl.pallas_call(
        pivot_kernel,
        in_specs=[smem, VMEM, VMEM, VMEM, ANY, ANY, ANY],
        out_specs=[VMEM, VMEM, ANY, ANY],
        out_shape=[half_shape, half_shape] + [shape_of(first)] * 2,
        scratch_shapes=[pltpu.VMEM((PW, own * BLOCK), F32)],
        input_output_aliases={5: 2, 6: 3},
        compiler_params=PARAMS,
        cost_estimate=SHORT,
        name="pivot",
    )(core, mine, slack_mine, diag, masked_done, second, beside)

    pair = kept + lax.ppermute(sent, "core", SWAP)
    pair = lax.all_to_all(pair.reshape(chips, 2 * PW // chips, BLOCK), ALL_CHIPS, 0, 0, tiled=True)
    opposite_beside = lax.ppermute(opposite, "z", SWAP)
    first_beside = lax.ppermute(beside, ("x", "core"), first_way)
    second_beside = lax.ppermute(beside, ("x", "core"), second_way)
    slack_rows = slack.reshape(own * blocks, BLOCK)
    near_pieces = with_other_core([piece, first, second, beside])
    schur, near_done = schur_product(masked, slack_rows, near_pieces, scens, 0, masked_done)

    share, first_beside, second_beside, opposite_beside = pl.pallas_call(
        total_kernel,
        in_specs=[VMEM] + [ANY] * 4,
        out_specs=[VMEM] + [ANY] * 3,
        out_shape=[shape_of(v) for v in (pair, first_beside, second_beside, opposite_beside)],
        input_output_aliases={2: 1, 3: 2, 4: 3},
        compiler_params=PARAMS,
        cost_estimate=SHORT,
        name="total",
    )(pair, near_done, first_beside, second_beside, opposite_beside)
    half = lax.all_to_all(share, ALL_CHIPS, 0, 0, tiled=True).reshape(2, PW, BLOCK)
    far_pieces = with_other_core([first_beside, second_beside, opposite, opposite_beside])
    schur, far_done = schur_product(masked, slack_rows, far_pieces, scens, 1, schur)
    half = follow(far_done, half)
    other = lax.ppermute(half, "core", SWAP)

    x, z = lax.axis_index("x"), lax.axis_index("z")
    order = []
    for step, side in ((0, 0), (-1, 0), (1, 0), (0, 1), (-1, 1), (1, 1), (2, 0), (2, 1)):
        for other_core in range(2):
            c = core_index if other_core == 0 else 1 - core_index
            chip_x = lax.rem(x + along + step * (1 - 2 * c), along)
            order.append((chip_x * 2 + lax.rem(z + side, 2)) * 2 + c)
    order = jnp.stack(order).astype(jnp.int32)
    pieces = near_pieces + far_pieces
    fwd, sol = pl.pallas_call(
        solve_kernel,
        grid=(1,),
        in_specs=[
            smem,
            smem,
            pl.BlockSpec((2, PW, BLOCK), lambda t: (0, 0, 0)),
            pl.BlockSpec((2, PW, BLOCK), lambda t: (0, 0, 0)),
        ]
        + [pl.BlockSpec((2, width, BLOCK), lambda t: (own * blocks // 2, 0, 0))] * len(pieces)
        + [ANY],
        out_specs=[pl.BlockSpec((PW, nrhs), lambda t: (0, 0))] * 2,
        out_shape=[jax.ShapeDtypeStruct((PW, nrhs), F32)] * 2,
        scratch_shapes=[
            pltpu.VMEM((PW, PW + nrhs), F32),
            pltpu.VMEM((BLOCK, 2 * BLOCK), F32),
            pltpu.VMEM((PW // BLOCK, BLOCK, BLOCK), F32),
        ],
        compiler_params=WIDE_PARAMS,
        cost_estimate=SHORT,
        name="solve",
    )(core, order, half, other, *pieces, far_done)
    schur = lax.all_to_all(schur, "scen", 0, 0, tiled=True)

    directions = pl.pallas_call(
        directions_kernel,
        in_specs=[VMEM] * 4,
        out_specs=VMEM,
        out_shape=shape_of(scen_rhs),
        compiler_params=WIDE_PARAMS,
        cost_estimate=SHORT,
        name="directions",
    )(sol, mine, slack_mine, scen_rhs)

    place = jnp.stack([scen_index, col_index]).astype(jnp.int32)
    own_share = own_width // scens
    reduced = pl.pallas_call(
        reduced_kernel,
        grid_spec=pltpu.PrefetchScalarGridSpec(
            num_scalar_prefetch=2,
            grid=(1,),
            in_specs=[
                pl.BlockSpec(schur.shape, lambda t, *_: (0, 0, 0)),
                pl.BlockSpec((PW, nrhs), lambda t, *_: (0, 0)),
                pl.BlockSpec((PW, nrhs), lambda t, *_: (0, 0)),
                pl.BlockSpec((own_share, nrhs), lambda t, place, *_: (place[0], 0)),
            ],
            out_specs=pl.BlockSpec((1, own_share, nrhs), lambda t, *_: (0, 0, 0)),
            scratch_shapes=[pltpu.VMEM((PW, nrhs), F32)],
        ),
        out_shape=jax.ShapeDtypeStruct((1, own_share, nrhs), F32),
        compiler_params=WIDE_PARAMS,
        cost_estimate=SHORT,
        name="reduced",
    )(place, order, schur, sol, fwd, rhs)
    return reduced, directions


def solution(mesh):
    scens, cols = mesh.devices.shape
    parts = Mesh(mesh.devices.reshape(scens, cols // 4, 2, 2), ("scen", "x", "z", "core"))
    return jax.shard_map(
        per_device,
        mesh=parts,
        in_specs=(
            P("scen", None, COL),
            P("scen", None, COL),
            P("scen", None),
            P(COL),
            P(COL, None),
            P("scen", COL, None),
        ),
        out_specs=(P(COL, "scen", None), P("scen", COL, None)),
        check_vma=False,
    )
```

```python
import jax
import jax.numpy as jnp
from jax import lax
from jax.experimental import pallas as pl
from jax.experimental.pallas import tpu as pltpu
from jax.sharding import Mesh, PartitionSpec as P

PW = 512
BLOCK = 128
SLAB = 8
STEPS = 8
F32 = jnp.float32
BF16 = jnp.bfloat16
COL = ("x", "z", "core")
SWAP = [(0, 1), (1, 0)]
ALL_CHIPS = ("scen", "x", "z")
DONE = jax.ShapeDtypeStruct((8, 128), F32)
DONE_SPEC = pl.BlockSpec((8, 128), lambda t: (0, 0))
ANY = pl.BlockSpec(memory_space=pl.ANY)
VMEM = pl.BlockSpec(memory_space=pltpu.VMEM)
PARAMS = pltpu.CompilerParams(vmem_limit_bytes=20 << 20)
SHORT = pl.CostEstimate(flops=1 << 20, bytes_accessed=1 << 16, transcendentals=0)
WIDE_PARAMS = pltpu.CompilerParams(vmem_limit_bytes=56 << 20)


def dot(a, b, dims, precision=lax.Precision.HIGHEST):
    return lax.dot_general(a, b, (dims, ((), ())), precision=precision, preferred_element_type=F32)


def dot_nn(a, b):
    return dot(a, b, ((1,), (0,)))


def dot_tn(a, b):
    return dot(a, b, ((0,), (0,)))


def dot_nt(a, b):
    return dot(a, b, ((1,), (1,)))


def panel_kernel(pattern, border, rhs, row_out, all_out):
    scen = pl.program_id(0)
    width = rhs.shape[0]
    blocks = row_out.shape[0]
    for i in range(blocks):
        rows = border[0, i * BLOCK : (i + 1) * BLOCK, :].T[:width]
        rows = rows * pattern[scen, 0, i].astype(F32)
        row_out[i, 0] = rows
        all_out[scen * blocks + i] = rows

    @pl.when(scen == 0)
    def _():
        for h in range(2):
            all_out[2 * blocks + h] = rhs[:, h * BLOCK : (h + 1) * BLOCK]


def pivot_kernel(core, mine, slack, diag, *refs):
    kept, sent, right = refs[3], refs[4], refs[-1]
    size = diag.shape[1]
    for s in range(2):
        right[:, s * BLOCK : (s + 1) * BLOCK] = mine[:, s].reshape(size, BLOCK)
    left = jnp.concatenate([right[:, s * BLOCK : (s + 1) * BLOCK] / slack[s : s + 1, :] for s in range(2)], axis=1)
    rows = lax.broadcasted_iota(jnp.int32, (size, BLOCK), 0)
    cols = lax.broadcasted_iota(jnp.int32, (size, BLOCK), 1)
    for out, place in ((kept, core[0]), (sent, 1 - core[0])):
        for q in range(2):
            first = pl.multiple_of((q + 2 * place) * BLOCK, BLOCK)
            piece = dot_nt(left, right[pl.ds(first, BLOCK), :])
            out[q] = piece + jnp.where(rows == cols + first, diag[:, pl.ds(first, BLOCK)], 0.0)


def total_kernel(pair, *refs):
    shared = refs[4]
    total = pair[0]
    for k in range(1, pair.shape[0]):
        total = total + pair[k]
    for k in range(pair.shape[0]):
        shared[k] = total


def split(values):
    high = values.astype(BF16)
    return high, (values - high.astype(F32)).astype(BF16)


def mask_kernel(pattern, border, _, out, done):
    step = pl.program_id(0)
    done[...] = jnp.zeros_like(done)
    depth, width = border.shape[1:]
    per_scen = STEPS // pattern.shape[0]
    for e in range(depth // BLOCK):
        block = lax.rem(step, per_scen) * (depth // BLOCK) + e
        at = e * BLOCK
        for c in range(width // BLOCK):
            lanes = slice(c * BLOCK, (c + 1) * BLOCK)
            weight = pattern[lax.div(step, per_scen), c, block].astype(F32)
            high, low = split(border[0, at : at + BLOCK, lanes] * weight)
            out[0, at : at + BLOCK, lanes] = high
            out[0, depth + at : depth + at + BLOCK, lanes] = low


def mask_parts(pattern, border, after):
    scenarios, row_total, own_width = border.shape
    depth = scenarios * row_total // STEPS
    per_scen = row_total // depth
    return pl.pallas_call(
        mask_kernel,
        grid=(STEPS,),
        in_specs=[
            pl.BlockSpec(memory_space=pltpu.SMEM),
            pl.BlockSpec((1, depth, own_width), lambda t: (t // per_scen, t % per_scen, 0)),
            ANY,
        ],
        out_specs=[pl.BlockSpec((1, 2 * depth, own_width), lambda t: (t, 0, 0)), DONE_SPEC],
        out_shape=[jax.ShapeDtypeStruct((STEPS, 2 * depth, own_width), BF16), DONE],
        compiler_params=WIDE_PARAMS,
        cost_estimate=SHORT,
        name="mask",
    )(pattern, border, after)


def follow_kernel(*refs):
    del refs


def follow(first, value):
    return pl.pallas_call(
        follow_kernel,
        in_specs=[ANY, ANY],
        out_specs=ANY,
        out_shape=shape_of(value),
        input_output_aliases={1: 0},
        compiler_params=PARAMS,
        cost_estimate=SHORT,
        name="follow",
    )(first, value)


def schur_kernel(masked, slack, _, *refs):
    *pieces, out, done, high, low, held, sems = refs
    step = pl.program_id(0)
    depth = masked.shape[1] // 2
    blocks, width = held.shape[1:3]

    @pl.when(step == 0)
    def _():
        done[...] = jnp.zeros_like(done)
        out[...] = jnp.zeros_like(out)
        copies = [
            pltpu.make_async_copy(piece.at[pl.ds(0, blocks)], held.at[k], sems.at[k]) for k, piece in enumerate(pieces)
        ]
        for copy in copies:
            copy.start()
        for k, copy in enumerate(copies):
            copy.wait()

            def prepare(e, carry):
                inverse = 1.0 / slack[pl.ds(e, 1), :]
                lanes = pl.ds(pl.multiple_of(e * BLOCK, BLOCK), BLOCK)
                rows = slice(k * width, (k + 1) * width)
                high[rows, lanes], low[rows, lanes] = split(held[k, e] * inverse)
                return carry

            lax.fori_loop(0, blocks, prepare, 0, unroll=4)

    now = pl.ds(pl.multiple_of(step * depth, depth), depth)
    dims = ((1,), (0,))
    wide = 2 * BLOCK
    for n in range(masked.shape[2] // wide):
        lanes = slice(n * wide, (n + 1) * wide)
        product = dot(high[:, now], masked[0, :depth, lanes], dims, lax.Precision.DEFAULT)
        product += dot(high[:, now], masked[0, depth:, lanes], dims, lax.Precision.DEFAULT)
        product += dot(low[:, now], masked[0, :depth, lanes], dims, lax.Precision.DEFAULT)
        out[2 * n] += product[:, :BLOCK]
        out[2 * n + 1] += product[:, BLOCK:]


def schur_product(masked, slack, pieces, scens, part, earlier):
    steps, depth, own_width = masked.shape
    width = pieces[0].shape[1]
    rows = len(pieces) * width
    total = steps * depth // 2
    shape = (scens, rows, own_width // scens)
    return pl.pallas_call(
        schur_kernel,
        grid=(steps,),
        in_specs=[
            pl.BlockSpec((1, depth, own_width), lambda t: (t, 0, 0)),
            pl.BlockSpec(slack.shape, lambda t: (0, 0)),
        ]
        + [ANY] * (1 + len(pieces)),
        out_specs=[pl.BlockSpec(shape, lambda t: (0, part, 0)), DONE_SPEC],
        out_shape=[jax.ShapeDtypeStruct((scens, 2 * rows, own_width // scens), F32), DONE],
        input_output_aliases={2: 0} if part else {},
        scratch_shapes=[
            pltpu.VMEM((rows, total), BF16),
            pltpu.VMEM((rows, total), BF16),
            pltpu.VMEM((len(pieces), total // BLOCK, width, BLOCK), F32),
            pltpu.SemaphoreType.DMA((len(pieces),)),
        ],
        compiler_params=WIDE_PARAMS,
        cost_estimate=SHORT,
        name="schur",
    )(masked, slack, earlier, *pieces)


def eliminate(w):
    for first in range(0, BLOCK, SLAB):
        height = BLOCK - first
        cols = [jnp.broadcast_to(w[first:, first + k : first + k + 1], (height, BLOCK)) for k in range(SLAB)]
        left, right = w[first : first + SLAB, :BLOCK], w[first : first + SLAB, BLOCK:]
        lower, upper = [], []
        for k in range(SLAB):
            scale = lax.rsqrt(cols[k][k : k + 1, :])
            square = scale * scale
            for m in range(k + 1, SLAB):
                cols[m] = cols[m] - cols[k] * (cols[k][m : m + 1, :] * square)
            low = cols[k] * scale
            u0 = left[k : k + 1, :] * scale
            u1 = right[k : k + 1, :] * scale
            if k + 1 < SLAB:
                left = left - low[:SLAB] * u0
                right = right - low[:SLAB] * u1
            w[first + k : first + k + 1, BLOCK:] = u1
            lower.append(low)
            upper.append((u0, u1))
        if height > SLAB:
            rest0, rest1 = w[first + SLAB :, :BLOCK], w[first + SLAB :, BLOCK:]
            for k in range(SLAB):
                rest0 = rest0 - lower[k][SLAB:] * upper[k][0]
                rest1 = rest1 - lower[k][SLAB:] * upper[k][1]
            w[first + SLAB :, :BLOCK] = rest0
            w[first + SLAB :, BLOCK:] = rest1


def rows_of(order, k, width):
    return pl.ds(pl.multiple_of(order[k] * width, width), width)


def solve_kernel(core, order, mine, other, *refs):
    *pieces, _, fwd, sol, m, w, linv = refs
    size = fwd.shape[0]
    steps = size // BLOCK
    width = pieces[0].shape[1]
    for q in range(2):
        here = pl.ds(pl.multiple_of((q + 2 * core[0]) * BLOCK, BLOCK), BLOCK)
        m[:, here] = mine[q]
        here = pl.ds(pl.multiple_of((q + 2 * (1 - core[0])) * BLOCK, BLOCK), BLOCK)
        m[:, here] = other[q]
        for k, piece in enumerate(pieces):
            m[rows_of(order, k, width), size + q * BLOCK : size + (q + 1) * BLOCK] = piece[q]
    shape = (BLOCK, BLOCK)
    eye = (lax.broadcasted_iota(jnp.int32, shape, 0) == lax.broadcasted_iota(jnp.int32, shape, 1)).astype(F32)

    def outer(step, carry):
        here = pl.ds(pl.multiple_of(step * BLOCK, BLOCK), BLOCK)
        w[:, :BLOCK] = m[here, here]
        w[:, BLOCK:] = eye
        eliminate(w)
        inverse = w[:, BLOCK:]
        linv[step] = inverse
        m[here, :] = dot_nn(inverse, m[here, :])

        def update(later, inner):
            there = pl.ds(pl.multiple_of(later * BLOCK, BLOCK), BLOCK)
            m[there, :] = m[there, :] - dot_tn(m[here, there], m[here, :])
            return inner

        lax.fori_loop(step + 1, steps, update, 0)
        return carry

    lax.fori_loop(0, steps, outer, 0)
    fwd[...] = m[:, size:]
    for step in reversed(range(steps)):
        rows = slice(step * BLOCK, (step + 1) * BLOCK)
        total = m[rows, size:]
        if step + 1 < steps:
            after = (step + 1) * BLOCK
            total = total - dot_nn(m[rows, after:size], sol[after:, :])
        sol[rows, :] = dot_tn(linv[step], total)


def directions_kernel(sol, mine, slack, scen_rhs, directions):
    size = sol.shape[0]
    solved = sol[...]
    for s in range(2):
        moved = dot_tn(mine[:, s].reshape(size, BLOCK), solved)
        divisor = jnp.broadcast_to(slack[s : s + 1, :], (BLOCK, BLOCK)).T
        for h in range(moved.shape[1] // BLOCK):
            lanes = slice(h * BLOCK, (h + 1) * BLOCK)
            directions[s, :, lanes] = (scen_rhs[s, :, lanes] - moved[:, lanes]) / divisor


def reduced_kernel(place, order, schur, sol, fwd, rhs, reduced, moved_sol):
    pieces = order.shape[0]
    width = sol.shape[0] // pieces
    for k in range(pieces):
        moved_sol[k * width : (k + 1) * width, :] = sol[rows_of(order, k, width), :]
    total = schur[0]
    for k in range(1, schur.shape[0]):
        total = total + schur[k]
    reduced[0] = rhs[...] - dot_tn(total, moved_sol[...])

    @pl.when(place[0] == 0)
    def _():
        reduced[0, :width] = fwd[rows_of(place, 1, width), :]


def shape_of(value):
    return jax.ShapeDtypeStruct(value.shape, value.dtype)


def with_other_core(pieces):
    return [value for piece in pieces for value in (piece, lax.ppermute(piece, "core", SWAP))]


def per_device(border, pattern, slack, first_diag, rhs, scen_rhs):
    scen_index = lax.axis_index("scen")
    core_index = lax.axis_index("core")
    pattern = jnp.transpose(pattern, (0, 2, 1))
    col_index = lax.axis_index(COL)
    cols = lax.axis_size(COL)
    scens = lax.axis_size("scen")
    chips = lax.axis_size(ALL_CHIPS)
    own, row_total, own_width = border.shape
    width = PW // cols
    nrhs = rhs.shape[1]
    blocks = row_total // BLOCK
    smem = pl.BlockSpec(memory_space=pltpu.SMEM)

    row_blocks, piece = pl.pallas_call(
        panel_kernel,
        grid=(own,),
        in_specs=[
            smem,
            pl.BlockSpec((1, row_total, BLOCK), lambda s: (s, 0, 0)),
            pl.BlockSpec((width, nrhs), lambda s: (0, 0)),
        ],
        out_specs=[
            pl.BlockSpec((blocks, 1, width, BLOCK), lambda s: (0, s, 0, 0)),
            pl.BlockSpec((own * blocks + 2, width, BLOCK), lambda s: (0, 0, 0)),
        ],
        out_shape=[
            jax.ShapeDtypeStruct((blocks, own, width, BLOCK), F32),
            jax.ShapeDtypeStruct((own * blocks + 2, width, BLOCK), F32),
        ],
        compiler_params=WIDE_PARAMS,
        name="panel",
    )(pattern, border, rhs)

    mine = lax.all_to_all(row_blocks, COL, 0, 0, tiled=True)
    along = lax.axis_size("x")
    first_way = [(2 * a + c, 2 * ((a + 1 - 2 * c) % along) + c) for a in range(along) for c in range(2)]
    second_way = [(target, source) for source, target in first_way]
    first = lax.ppermute(piece, ("x", "core"), first_way)
    second = lax.ppermute(piece, ("x", "core"), second_way)
    beside = lax.ppermute(piece, "z", SWAP)
    masked, masked_done = mask_parts(pattern, border, row_blocks)
    first = follow(masked_done, first)
    opposite = lax.ppermute(first, ("x", "core"), first_way)

    slack_mine = lax.dynamic_slice_in_dim(slack, col_index * BLOCK, BLOCK, 1)
    diag = jnp.where(scen_index == 0, first_diag[:width], 0.0)
    diag = lax.dynamic_update_slice_in_dim(jnp.zeros((PW,), F32), diag, col_index * width, 0).reshape(1, PW)
    core = core_index.reshape(1).astype(jnp.int32)
    half_shape = jax.ShapeDtypeStruct((2, PW, BLOCK), F32)
    kept, sent, second, beside = pl.pallas_call(
        pivot_kernel,
        in_specs=[smem, VMEM, VMEM, VMEM, ANY, ANY, ANY],
        out_specs=[VMEM, VMEM, ANY, ANY],
        out_shape=[half_shape, half_shape] + [shape_of(first)] * 2,
        scratch_shapes=[pltpu.VMEM((PW, own * BLOCK), F32)],
        input_output_aliases={5: 2, 6: 3},
        compiler_params=PARAMS,
        cost_estimate=SHORT,
        name="pivot",
    )(core, mine, slack_mine, diag, masked_done, second, beside)

    pair = kept + lax.ppermute(sent, "core", SWAP)
    pair = lax.all_to_all(pair.reshape(chips, 2 * PW // chips, BLOCK), ALL_CHIPS, 0, 0, tiled=True)
    opposite_beside = lax.ppermute(opposite, "z", SWAP)
    first_beside = lax.ppermute(beside, ("x", "core"), first_way)
    second_beside = lax.ppermute(beside, ("x", "core"), second_way)
    slack_rows = slack.reshape(own * blocks, BLOCK)
    near_pieces = with_other_core([piece, first, second, beside])
    schur, near_done = schur_product(masked, slack_rows, near_pieces, scens, 0, masked_done)

    share, first_beside, second_beside, opposite_beside = pl.pallas_call(
        total_kernel,
        in_specs=[VMEM] + [ANY] * 4,
        out_specs=[VMEM] + [ANY] * 3,
        out_shape=[shape_of(v) for v in (pair, first_beside, second_beside, opposite_beside)],
        input_output_aliases={2: 1, 3: 2, 4: 3},
        compiler_params=PARAMS,
        cost_estimate=SHORT,
        name="total",
    )(pair, near_done, first_beside, second_beside, opposite_beside)
    half = lax.all_to_all(share, ALL_CHIPS, 0, 0, tiled=True).reshape(2, PW, BLOCK)
    far_pieces = with_other_core([first_beside, second_beside, opposite, opposite_beside])
    schur, far_done = schur_product(masked, slack_rows, far_pieces, scens, 1, schur)
    half = follow(far_done, half)
    other = lax.ppermute(half, "core", SWAP)

    x, z = lax.axis_index("x"), lax.axis_index("z")
    order = []
    for step, side in ((0, 0), (-1, 0), (1, 0), (0, 1), (-1, 1), (1, 1), (2, 0), (2, 1)):
        for other_core in range(2):
            c = core_index if other_core == 0 else 1 - core_index
            chip_x = lax.rem(x + along + step * (1 - 2 * c), along)
            order.append((chip_x * 2 + lax.rem(z + side, 2)) * 2 + c)
    order = jnp.stack(order).astype(jnp.int32)
    pieces = near_pieces + far_pieces
    fwd, sol = pl.pallas_call(
        solve_kernel,
        grid=(1,),
        in_specs=[
            smem,
            smem,
            pl.BlockSpec((2, PW, BLOCK), lambda t: (0, 0, 0)),
            pl.BlockSpec((2, PW, BLOCK), lambda t: (0, 0, 0)),
        ]
        + [pl.BlockSpec((2, width, BLOCK), lambda t: (own * blocks // 2, 0, 0))] * len(pieces)
        + [ANY],
        out_specs=[pl.BlockSpec((PW, nrhs), lambda t: (0, 0))] * 2,
        out_shape=[jax.ShapeDtypeStruct((PW, nrhs), F32)] * 2,
        scratch_shapes=[
            pltpu.VMEM((PW, PW + nrhs), F32),
            pltpu.VMEM((BLOCK, 2 * BLOCK), F32),
            pltpu.VMEM((PW // BLOCK, BLOCK, BLOCK), F32),
        ],
        compiler_params=WIDE_PARAMS,
        cost_estimate=SHORT,
        name="solve",
    )(core, order, half, other, *pieces, far_done)
    schur = lax.all_to_all(schur, "scen", 0, 0, tiled=True)

    directions = pl.pallas_call(
        directions_kernel,
        in_specs=[VMEM] * 4,
        out_specs=VMEM,
        out_shape=shape_of(scen_rhs),
        compiler_params=WIDE_PARAMS,
        cost_estimate=SHORT,
        name="directions",
    )(sol, mine, slack_mine, scen_rhs)

    place = jnp.stack([scen_index, col_index]).astype(jnp.int32)
    own_share = own_width // scens
    reduced = pl.pallas_call(
        reduced_kernel,
        grid_spec=pltpu.PrefetchScalarGridSpec(
            num_scalar_prefetch=2,
            grid=(1,),
            in_specs=[
                pl.BlockSpec(schur.shape, lambda t, *_: (0, 0, 0)),
                pl.BlockSpec((PW, nrhs), lambda t, *_: (0, 0)),
                pl.BlockSpec((PW, nrhs), lambda t, *_: (0, 0)),
                pl.BlockSpec((own_share, nrhs), lambda t, place, *_: (place[0], 0)),
            ],
            out_specs=pl.BlockSpec((1, own_share, nrhs), lambda t, *_: (0, 0, 0)),
            scratch_shapes=[pltpu.VMEM((PW, nrhs), F32)],
        ),
        out_shape=jax.ShapeDtypeStruct((1, own_share, nrhs), F32),
        compiler_params=WIDE_PARAMS,
        cost_estimate=SHORT,
        name="reduced",
    )(place, order, schur, sol, fwd, rhs)
    return reduced, directions


def solution(mesh):
    scens, cols = mesh.devices.shape
    parts = Mesh(mesh.devices.reshape(scens, cols // 4, 2, 2), ("scen", "x", "z", "core"))
    return jax.shard_map(
        per_device,
        mesh=parts,
        in_specs=(
            P("scen", None, COL),
            P("scen", None, COL),
            P("scen", None),
            P(COL),
            P(COL, None),
            P("scen", COL, None),
        ),
        out_specs=(P(COL, "scen", None), P("scen", COL, None)),
        check_vma=False,
    )
```

```python
import jax
import jax.numpy as jnp
from jax import lax
from jax.experimental import pallas as pl
from jax.experimental.pallas import tpu as pltpu
from jax.sharding import Mesh, PartitionSpec as P

PW = 512
BLOCK = 128
SLAB = 8
STEPS = 8
F32 = jnp.float32
BF16 = jnp.bfloat16
COL = ("x", "z", "core")
SWAP = [(0, 1), (1, 0)]
ALL_CHIPS = ("scen", "x", "z")
DONE = jax.ShapeDtypeStruct((8, 128), F32)
DONE_SPEC = pl.BlockSpec((8, 128), lambda t: (0, 0))
ANY = pl.BlockSpec(memory_space=pl.ANY)
VMEM = pl.BlockSpec(memory_space=pltpu.VMEM)
PARAMS = pltpu.CompilerParams(vmem_limit_bytes=20 << 20)
SHORT = pl.CostEstimate(flops=1 << 20, bytes_accessed=1 << 16, transcendentals=0)
WIDE_PARAMS = pltpu.CompilerParams(vmem_limit_bytes=56 << 20)


def dot(a, b, dims, precision=lax.Precision.HIGHEST):
    return lax.dot_general(a, b, (dims, ((), ())), precision=precision, preferred_element_type=F32)


def dot_nn(a, b):
    return dot(a, b, ((1,), (0,)))


def dot_tn(a, b):
    return dot(a, b, ((0,), (0,)))


def dot_nt(a, b):
    return dot(a, b, ((1,), (1,)))


def panel_kernel(pattern, border, rhs, row_out, all_out):
    scen = pl.program_id(0)
    width = rhs.shape[0]
    blocks = row_out.shape[0]
    for i in range(blocks):
        rows = border[0, i * BLOCK : (i + 1) * BLOCK, :].T[:width]
        rows = rows * pattern[scen, 0, i].astype(F32)
        row_out[i, 0] = rows
        all_out[scen * blocks + i] = rows

    @pl.when(scen == 0)
    def _():
        for h in range(2):
            all_out[2 * blocks + h] = rhs[:, h * BLOCK : (h + 1) * BLOCK]


def pivot_kernel(core, mine, slack, diag, *refs):
    kept, sent, right = refs[3], refs[4], refs[-1]
    size = diag.shape[1]
    for s in range(2):
        right[:, s * BLOCK : (s + 1) * BLOCK] = mine[:, s].reshape(size, BLOCK)
    left = jnp.concatenate([right[:, s * BLOCK : (s + 1) * BLOCK] / slack[s : s + 1, :] for s in range(2)], axis=1)
    rows = lax.broadcasted_iota(jnp.int32, (size, BLOCK), 0)
    cols = lax.broadcasted_iota(jnp.int32, (size, BLOCK), 1)
    for out, place in ((kept, core[0]), (sent, 1 - core[0])):
        for q in range(2):
            first = pl.multiple_of((q + 2 * place) * BLOCK, BLOCK)
            piece = dot_nt(left, right[pl.ds(first, BLOCK), :])
            out[q] = piece + jnp.where(rows == cols + first, diag[:, pl.ds(first, BLOCK)], 0.0)


def total_kernel(pair, *refs):
    shared = refs[4]
    total = pair[0]
    for k in range(1, pair.shape[0]):
        total = total + pair[k]
    for k in range(pair.shape[0]):
        shared[k] = total


def split(values):
    high = values.astype(BF16)
    return high, (values - high.astype(F32)).astype(BF16)


def mask_kernel(pattern, border, _, out, done):
    step = pl.program_id(0)
    done[...] = jnp.zeros_like(done)
    depth, width = border.shape[1:]
    per_scen = STEPS // pattern.shape[0]
    for e in range(depth // BLOCK):
        block = lax.rem(step, per_scen) * (depth // BLOCK) + e
        at = e * BLOCK
        for c in range(width // BLOCK):
            lanes = slice(c * BLOCK, (c + 1) * BLOCK)
            weight = pattern[lax.div(step, per_scen), c, block].astype(F32)
            high, low = split(border[0, at : at + BLOCK, lanes] * weight)
            out[0, at : at + BLOCK, lanes] = high
            out[0, depth + at : depth + at + BLOCK, lanes] = low


def mask_parts(pattern, border, after):
    scenarios, row_total, own_width = border.shape
    depth = scenarios * row_total // STEPS
    per_scen = row_total // depth
    return pl.pallas_call(
        mask_kernel,
        grid=(STEPS,),
        in_specs=[
            pl.BlockSpec(memory_space=pltpu.SMEM),
            pl.BlockSpec((1, depth, own_width), lambda t: (t // per_scen, t % per_scen, 0)),
            ANY,
        ],
        out_specs=[pl.BlockSpec((1, 2 * depth, own_width), lambda t: (t, 0, 0)), DONE_SPEC],
        out_shape=[jax.ShapeDtypeStruct((STEPS, 2 * depth, own_width), BF16), DONE],
        compiler_params=WIDE_PARAMS,
        cost_estimate=SHORT,
        name="mask",
    )(pattern, border, after)


def follow_kernel(*refs):
    del refs


def follow(first, value):
    return pl.pallas_call(
        follow_kernel,
        in_specs=[ANY, ANY],
        out_specs=ANY,
        out_shape=shape_of(value),
        input_output_aliases={1: 0},
        compiler_params=PARAMS,
        cost_estimate=SHORT,
        name="follow",
    )(first, value)


def schur_kernel(masked, slack, _, *refs):
    *pieces, out, done, left = refs
    step = pl.program_id(0)
    done[...] = jnp.zeros_like(done)
    count, width = pieces[0].shape[:2]
    depth = count * BLOCK
    per_scen = slack.shape[1] // depth
    for e in range(count):
        at = e * BLOCK
        first = pl.multiple_of(lax.rem(step, per_scen) * depth + at, BLOCK)
        both = slack[:, pl.ds(first, BLOCK)]
        inverse = 1.0 / jnp.where(step < per_scen, both[0:1], both[1:2])
        for k, piece in enumerate(pieces):
            high, low = split(piece[e] * inverse)
            rows = slice(k * width, (k + 1) * width)
            left[rows, at : at + BLOCK] = high
            left[rows, depth + at : depth + at + BLOCK] = high
            left[rows, 2 * depth + at : 2 * depth + at + BLOCK] = low

    @pl.when(step == 0)
    def _():
        out[...] = jnp.zeros_like(out)

    wide = 2 * BLOCK
    dims = ((1,), (0,))
    for n in range(masked.shape[2] // wide):
        lanes = slice(n * wide, (n + 1) * wide)
        product = dot(left[:, : 2 * depth], masked[0, :, lanes], dims, lax.Precision.DEFAULT)
        product += dot(left[:, 2 * depth :], masked[0, :depth, lanes], dims, lax.Precision.DEFAULT)
        out[2 * n] += product[:, :BLOCK]
        out[2 * n + 1] += product[:, BLOCK:]


def schur_product(masked, slack, pieces, scens, part, earlier):
    steps, depth, own_width = masked.shape
    depth //= 2
    width = pieces[0].shape[1]
    rows = len(pieces) * width
    shape = (scens, rows, own_width // scens)
    return pl.pallas_call(
        schur_kernel,
        grid=(steps,),
        in_specs=[
            pl.BlockSpec((1, 2 * depth, own_width), lambda t: (t, 0, 0)),
            pl.BlockSpec(slack.shape, lambda t: (0, 0)),
            ANY,
        ]
        + [pl.BlockSpec((depth // BLOCK, width, BLOCK), lambda t: (t, 0, 0))] * len(pieces),
        out_specs=[pl.BlockSpec(shape, lambda t: (0, part, 0)), DONE_SPEC],
        out_shape=[jax.ShapeDtypeStruct((scens, 2 * rows, own_width // scens), F32), DONE],
        input_output_aliases={2: 0} if part else {},
        scratch_shapes=[pltpu.VMEM((rows, 3 * depth), BF16)],
        compiler_params=WIDE_PARAMS,
        cost_estimate=SHORT,
        name="schur",
    )(masked, slack, earlier, *pieces)


def eliminate(w):
    for first in range(0, BLOCK, SLAB):
        height = BLOCK - first
        cols = [jnp.broadcast_to(w[first:, first + k : first + k + 1], (height, BLOCK)) for k in range(SLAB)]
        left, right = w[first : first + SLAB, :BLOCK], w[first : first + SLAB, BLOCK:]
        lower, upper = [], []
        for k in range(SLAB):
            pivot = cols[k][k : k + 1, :]
            scale = lax.rsqrt(pivot)
            inverse = 1.0 / pivot
            for m in range(k + 1, SLAB):
                cols[m] = cols[m] - cols[k] * (cols[k][m : m + 1, :] * inverse)
            low = cols[k] * scale
            u0 = left[k : k + 1, :] * scale
            u1 = right[k : k + 1, :] * scale
            if k + 1 < SLAB:
                left = left - low[:SLAB] * u0
                right = right - low[:SLAB] * u1
            w[first + k : first + k + 1, BLOCK:] = u1
            lower.append(low)
            upper.append((u0, u1))
        if height > SLAB:
            rest0, rest1 = w[first + SLAB :, :BLOCK], w[first + SLAB :, BLOCK:]
            for k in range(SLAB):
                rest0 = rest0 - lower[k][SLAB:] * upper[k][0]
                rest1 = rest1 - lower[k][SLAB:] * upper[k][1]
            w[first + SLAB :, :BLOCK] = rest0
            w[first + SLAB :, BLOCK:] = rest1


def rows_of(order, k, width):
    return pl.ds(pl.multiple_of(order[k] * width, width), width)


def solve_kernel(core, order, mine, other, *refs):
    *pieces, _, fwd, sol, m, w, linv = refs
    size = fwd.shape[0]
    steps = size // BLOCK
    width = pieces[0].shape[1]
    for q in range(2):
        here = pl.ds(pl.multiple_of((q + 2 * core[0]) * BLOCK, BLOCK), BLOCK)
        m[:, here] = mine[q]
        here = pl.ds(pl.multiple_of((q + 2 * (1 - core[0])) * BLOCK, BLOCK), BLOCK)
        m[:, here] = other[q]
        for k, piece in enumerate(pieces):
            m[rows_of(order, k, width), size + q * BLOCK : size + (q + 1) * BLOCK] = piece[q]
    shape = (BLOCK, BLOCK)
    eye = (lax.broadcasted_iota(jnp.int32, shape, 0) == lax.broadcasted_iota(jnp.int32, shape, 1)).astype(F32)

    for step in range(steps):
        after = (step + 1) * BLOCK
        here = slice(step * BLOCK, after)
        w[:, :BLOCK] = m[here, here]
        w[:, BLOCK:] = eye
        eliminate(w)
        inverse = w[:, BLOCK:]
        linv[step] = inverse
        m[here, after:] = dot_nn(inverse, m[here, after:])
        for later in range(step + 1, steps):
            first = later * BLOCK
            there = slice(first, first + BLOCK)
            m[there, first:] = m[there, first:] - dot_tn(m[here, there], m[here, first:])
    fwd[...] = m[:, size:]
    for step in reversed(range(steps)):
        rows = slice(step * BLOCK, (step + 1) * BLOCK)
        total = m[rows, size:]
        if step + 1 < steps:
            after = (step + 1) * BLOCK
            total = total - dot_nn(m[rows, after:size], sol[after:, :])
        sol[rows, :] = dot_tn(linv[step], total)


def directions_kernel(sol, mine, slack, scen_rhs, directions):
    size = sol.shape[0]
    solved = sol[...]
    for s in range(2):
        moved = dot_tn(mine[:, s].reshape(size, BLOCK), solved)
        divisor = jnp.broadcast_to(slack[s : s + 1, :], (BLOCK, BLOCK)).T
        for h in range(moved.shape[1] // BLOCK):
            lanes = slice(h * BLOCK, (h + 1) * BLOCK)
            directions[s, :, lanes] = (scen_rhs[s, :, lanes] - moved[:, lanes]) / divisor


def reduced_kernel(place, order, schur, sol, fwd, rhs, reduced, moved_sol):
    pieces = order.shape[0]
    width = sol.shape[0] // pieces
    for k in range(pieces):
        moved_sol[k * width : (k + 1) * width, :] = sol[rows_of(order, k, width), :]
    total = schur[0]
    for k in range(1, schur.shape[0]):
        total = total + schur[k]
    reduced[0] = rhs[...] - dot_tn(total, moved_sol[...])

    @pl.when(place[0] == 0)
    def _():
        reduced[0, :width] = fwd[rows_of(place, 1, width), :]


def shape_of(value):
    return jax.ShapeDtypeStruct(value.shape, value.dtype)


def with_other_core(pieces):
    return [value for piece in pieces for value in (piece, lax.ppermute(piece, "core", SWAP))]


def per_device(border, pattern, slack, first_diag, rhs, scen_rhs):
    scen_index = lax.axis_index("scen")
    core_index = lax.axis_index("core")
    pattern = jnp.transpose(pattern, (0, 2, 1))
    col_index = lax.axis_index(COL)
    cols = lax.axis_size(COL)
    scens = lax.axis_size("scen")
    chips = lax.axis_size(ALL_CHIPS)
    own, row_total, own_width = border.shape
    width = PW // cols
    nrhs = rhs.shape[1]
    blocks = row_total // BLOCK
    smem = pl.BlockSpec(memory_space=pltpu.SMEM)

    row_blocks, piece = pl.pallas_call(
        panel_kernel,
        grid=(own,),
        in_specs=[
            smem,
            pl.BlockSpec((1, row_total, BLOCK), lambda s: (s, 0, 0)),
            pl.BlockSpec((width, nrhs), lambda s: (0, 0)),
        ],
        out_specs=[
            pl.BlockSpec((blocks, 1, width, BLOCK), lambda s: (0, s, 0, 0)),
            pl.BlockSpec((own * blocks + 2, width, BLOCK), lambda s: (0, 0, 0)),
        ],
        out_shape=[
            jax.ShapeDtypeStruct((blocks, own, width, BLOCK), F32),
            jax.ShapeDtypeStruct((own * blocks + 2, width, BLOCK), F32),
        ],
        compiler_params=WIDE_PARAMS,
        name="panel",
    )(pattern, border, rhs)

    mine = lax.all_to_all(row_blocks, COL, 0, 0, tiled=True)
    along = lax.axis_size("x")
    first_way = [(2 * a + c, 2 * ((a + 1 - 2 * c) % along) + c) for a in range(along) for c in range(2)]
    second_way = [(target, source) for source, target in first_way]
    first = lax.ppermute(piece, ("x", "core"), first_way)
    second = lax.ppermute(piece, ("x", "core"), second_way)
    beside = lax.ppermute(piece, "z", SWAP)
    masked, masked_done = mask_parts(pattern, border, row_blocks)
    first = follow(masked_done, first)
    opposite = lax.ppermute(first, ("x", "core"), first_way)

    slack_mine = lax.dynamic_slice_in_dim(slack, col_index * BLOCK, BLOCK, 1)
    diag = jnp.where(scen_index == 0, first_diag[:width], 0.0)
    diag = lax.dynamic_update_slice_in_dim(jnp.zeros((PW,), F32), diag, col_index * width, 0).reshape(1, PW)
    core = core_index.reshape(1).astype(jnp.int32)
    half_shape = jax.ShapeDtypeStruct((2, PW, BLOCK), F32)
    kept, sent, second, beside = pl.pallas_call(
        pivot_kernel,
        in_specs=[smem, VMEM, VMEM, VMEM, ANY, ANY, ANY],
        out_specs=[VMEM, VMEM, ANY, ANY],
        out_shape=[half_shape, half_shape] + [shape_of(first)] * 2,
        scratch_shapes=[pltpu.VMEM((PW, own * BLOCK), F32)],
        input_output_aliases={5: 2, 6: 3},
        compiler_params=PARAMS,
        cost_estimate=SHORT,
        name="pivot",
    )(core, mine, slack_mine, diag, masked_done, second, beside)

    pair = kept + lax.ppermute(sent, "core", SWAP)
    pair = lax.all_to_all(pair.reshape(chips, 2 * PW // chips, BLOCK), ALL_CHIPS, 0, 0, tiled=True)
    opposite_beside = lax.ppermute(opposite, "z", SWAP)
    first_beside = lax.ppermute(beside, ("x", "core"), first_way)
    second_beside = lax.ppermute(beside, ("x", "core"), second_way)
    near_pieces = with_other_core([piece, first, second, beside])
    schur, near_done = schur_product(masked, slack, near_pieces, scens, 0, masked_done)

    share, first_beside, second_beside, opposite_beside = pl.pallas_call(
        total_kernel,
        in_specs=[VMEM, ANY] + [ANY] * 3,
        out_specs=[VMEM] + [ANY] * 3,
        out_shape=[shape_of(v) for v in (pair, first_beside, second_beside, opposite_beside)],
        input_output_aliases={2: 1, 3: 2, 4: 3},
        compiler_params=PARAMS,
        cost_estimate=SHORT,
        name="total",
    )(pair, near_done, first_beside, second_beside, opposite_beside)
    half = lax.all_to_all(share, ALL_CHIPS, 0, 0, tiled=True).reshape(2, PW, BLOCK)
    far_pieces = with_other_core([first_beside, second_beside, opposite, opposite_beside])
    schur, far_done = schur_product(masked, slack, far_pieces, scens, 1, schur)
    half = follow(far_done, half)
    other = lax.ppermute(half, "core", SWAP)

    x, z = lax.axis_index("x"), lax.axis_index("z")
    order = []
    for step, side in ((0, 0), (-1, 0), (1, 0), (0, 1), (-1, 1), (1, 1), (2, 0), (2, 1)):
        for other_core in range(2):
            c = core_index if other_core == 0 else 1 - core_index
            chip_x = lax.rem(x + along + step * (1 - 2 * c), along)
            order.append((chip_x * 2 + lax.rem(z + side, 2)) * 2 + c)
    order = jnp.stack(order).astype(jnp.int32)
    pieces = near_pieces + far_pieces
    fwd, sol = pl.pallas_call(
        solve_kernel,
        grid=(1,),
        in_specs=[
            smem,
            smem,
            pl.BlockSpec((2, PW, BLOCK), lambda t: (0, 0, 0)),
            pl.BlockSpec((2, PW, BLOCK), lambda t: (0, 0, 0)),
        ]
        + [pl.BlockSpec((2, width, BLOCK), lambda t: (own * blocks // 2, 0, 0))] * len(pieces)
        + [ANY],
        out_specs=[pl.BlockSpec((PW, nrhs), lambda t: (0, 0))] * 2,
        out_shape=[jax.ShapeDtypeStruct((PW, nrhs), F32)] * 2,
        scratch_shapes=[
            pltpu.VMEM((PW, PW + nrhs), F32),
            pltpu.VMEM((BLOCK, 2 * BLOCK), F32),
            pltpu.VMEM((PW // BLOCK, BLOCK, BLOCK), F32),
        ],
        compiler_params=WIDE_PARAMS,
        cost_estimate=SHORT,
        name="solve",
    )(core, order, half, other, *pieces, far_done)
    schur = lax.all_to_all(schur, "scen", 0, 0, tiled=True)

    directions = pl.pallas_call(
        directions_kernel,
        in_specs=[VMEM] * 4,
        out_specs=VMEM,
        out_shape=shape_of(scen_rhs),
        compiler_params=WIDE_PARAMS,
        cost_estimate=SHORT,
        name="directions",
    )(sol, mine, slack_mine, scen_rhs)

    place = jnp.stack([scen_index, col_index]).astype(jnp.int32)
    own_share = own_width // scens
    reduced = pl.pallas_call(
        reduced_kernel,
        grid_spec=pltpu.PrefetchScalarGridSpec(
            num_scalar_prefetch=2,
            grid=(1,),
            in_specs=[
                pl.BlockSpec(schur.shape, lambda t, *_: (0, 0, 0)),
                pl.BlockSpec((PW, nrhs), lambda t, *_: (0, 0)),
                pl.BlockSpec((PW, nrhs), lambda t, *_: (0, 0)),
                pl.BlockSpec((own_share, nrhs), lambda t, place, *_: (place[0], 0)),
            ],
            out_specs=pl.BlockSpec((1, own_share, nrhs), lambda t, *_: (0, 0, 0)),
            scratch_shapes=[pltpu.VMEM((PW, nrhs), F32)],
        ),
        out_shape=jax.ShapeDtypeStruct((1, own_share, nrhs), F32),
        compiler_params=WIDE_PARAMS,
        cost_estimate=SHORT,
        name="reduced",
    )(place, order, schur, sol, fwd, rhs)
    return reduced, directions


def solution(mesh):
    scens, cols = mesh.devices.shape
    parts = Mesh(mesh.devices.reshape(scens, cols // 4, 2, 2), ("scen", "x", "z", "core"))
    return jax.shard_map(
        per_device,
        mesh=parts,
        in_specs=(
            P("scen", None, COL),
            P("scen", None, COL),
            P("scen", None),
            P(COL),
            P(COL, None),
            P("scen", COL, None),
        ),
        out_specs=(P(COL, "scen", None), P("scen", COL, None)),
        check_vma=False,
    )
```

```python
import jax
import jax.numpy as jnp
from jax import lax
from jax.experimental import pallas as pl
from jax.experimental.pallas import tpu as pltpu
from jax.sharding import Mesh, PartitionSpec as P

PW = 512
BLOCK = 128
SLAB = 8
STEPS = 8
F32 = jnp.float32
BF16 = jnp.bfloat16
COL = ("x", "z", "core")
SWAP = [(0, 1), (1, 0)]
ALL_CHIPS = ("scen", "x", "z")
DONE = jax.ShapeDtypeStruct((8, 128), F32)
DONE_SPEC = pl.BlockSpec((8, 128), lambda t: (0, 0))
ANY = pl.BlockSpec(memory_space=pl.ANY)
VMEM = pl.BlockSpec(memory_space=pltpu.VMEM)
PARAMS = pltpu.CompilerParams(vmem_limit_bytes=20 << 20)
SHORT = pl.CostEstimate(flops=1 << 20, bytes_accessed=1 << 16, transcendentals=0)
WIDE_PARAMS = pltpu.CompilerParams(vmem_limit_bytes=56 << 20)


def dot(a, b, dims, precision=lax.Precision.HIGHEST):
    return lax.dot_general(a, b, (dims, ((), ())), precision=precision, preferred_element_type=F32)


def dot_nn(a, b):
    return dot(a, b, ((1,), (0,)))


def dot_tn(a, b):
    return dot(a, b, ((0,), (0,)))


def dot_nt(a, b):
    return dot(a, b, ((1,), (1,)))


def panel_kernel(pattern, border, rhs, row_out, all_out):
    scen = pl.program_id(0)
    width = rhs.shape[0]
    blocks = row_out.shape[0]
    for i in range(blocks):
        rows = border[0, i * BLOCK : (i + 1) * BLOCK, :].T[:width]
        rows = rows * pattern[scen, 0, i].astype(F32)
        row_out[i, 0] = rows
        all_out[scen * blocks + i] = rows

    @pl.when(scen == 0)
    def _():
        for h in range(2):
            all_out[2 * blocks + h] = rhs[:, h * BLOCK : (h + 1) * BLOCK]


def pivot_kernel(place, mine, slack, diag, *refs):
    kept, sent, right = refs[3], refs[4], refs[-1]
    size = diag.shape[1]
    for s in range(2):
        right[:, s * BLOCK : (s + 1) * BLOCK] = mine[:, s].reshape(size, BLOCK)
    own_slack = slack[:, pl.ds(pl.multiple_of(place[1] * BLOCK, BLOCK), BLOCK)]
    left = jnp.concatenate([right[:, s * BLOCK : (s + 1) * BLOCK] / own_slack[s : s + 1] for s in range(2)], axis=1)
    rows = lax.broadcasted_iota(jnp.int32, (size, BLOCK), 0)
    cols = lax.broadcasted_iota(jnp.int32, (size, BLOCK), 1)
    for out, core in ((kept, place[2]), (sent, 1 - place[2])):
        for q in range(2):
            first = pl.multiple_of((q + 2 * core) * BLOCK, BLOCK)
            piece = dot_nt(left, right[pl.ds(first, BLOCK), :])
            out[q] = piece + jnp.where(rows == cols + first, diag[:, pl.ds(first, BLOCK)], 0.0)


def total_kernel(pair, *refs):
    shared = refs[4]
    total = pair[0]
    for k in range(1, pair.shape[0]):
        total = total + pair[k]
    for k in range(pair.shape[0]):
        shared[k] = total


def split(values):
    high = values.astype(BF16)
    return high, (values - high.astype(F32)).astype(BF16)


def mask_kernel(pattern, border, _, out, done):
    step = pl.program_id(0)
    done[...] = jnp.zeros_like(done)
    depth, width = border.shape[1:]
    per_scen = STEPS // pattern.shape[0]
    for e in range(depth // BLOCK):
        block = lax.rem(step, per_scen) * (depth // BLOCK) + e
        at = e * BLOCK
        for c in range(width // BLOCK):
            lanes = slice(c * BLOCK, (c + 1) * BLOCK)
            weight = pattern[lax.div(step, per_scen), c, block].astype(F32)
            high, low = split(border[0, at : at + BLOCK, lanes] * weight)
            out[0, at : at + BLOCK, lanes] = high
            out[0, depth + at : depth + at + BLOCK, lanes] = low


def mask_parts(pattern, border, after):
    scenarios, row_total, own_width = border.shape
    depth = scenarios * row_total // STEPS
    per_scen = row_total // depth
    return pl.pallas_call(
        mask_kernel,
        grid=(STEPS,),
        in_specs=[
            pl.BlockSpec(memory_space=pltpu.SMEM),
            pl.BlockSpec((1, depth, own_width), lambda t: (t // per_scen, t % per_scen, 0)),
            ANY,
        ],
        out_specs=[pl.BlockSpec((1, 2 * depth, own_width), lambda t: (t, 0, 0)), DONE_SPEC],
        out_shape=[jax.ShapeDtypeStruct((STEPS, 2 * depth, own_width), BF16), DONE],
        compiler_params=WIDE_PARAMS,
        cost_estimate=SHORT,
        name="mask",
    )(pattern, border, after)


def follow_kernel(*refs):
    del refs


def follow(first, value):
    return pl.pallas_call(
        follow_kernel,
        in_specs=[ANY, ANY],
        out_specs=ANY,
        out_shape=shape_of(value),
        input_output_aliases={1: 0},
        compiler_params=PARAMS,
        cost_estimate=SHORT,
        name="follow",
    )(first, value)


def schur_kernel(masked, slack, _, *refs):
    *pieces, out, done, left = refs
    step = pl.program_id(0)
    done[...] = jnp.zeros_like(done)
    count, width = pieces[0].shape[:2]
    depth = count * BLOCK
    per_scen = slack.shape[1] // depth
    for e in range(count):
        at = e * BLOCK
        first = pl.multiple_of(lax.rem(step, per_scen) * depth + at, BLOCK)
        both = slack[:, pl.ds(first, BLOCK)]
        inverse = 1.0 / jnp.where(step < per_scen, both[0:1], both[1:2])
        for k, piece in enumerate(pieces):
            high, low = split(piece[e] * inverse)
            rows = slice(k * width, (k + 1) * width)
            left[rows, at : at + BLOCK] = high
            left[rows, depth + at : depth + at + BLOCK] = high
            left[rows, 2 * depth + at : 2 * depth + at + BLOCK] = low

    @pl.when(step == 0)
    def _():
        out[...] = jnp.zeros_like(out)

    wide = 2 * BLOCK
    dims = ((1,), (0,))
    for n in range(masked.shape[2] // wide):
        lanes = slice(n * wide, (n + 1) * wide)
        product = dot(left[:, : 2 * depth], masked[0, :, lanes], dims, lax.Precision.DEFAULT)
        product += dot(left[:, 2 * depth :], masked[0, :depth, lanes], dims, lax.Precision.DEFAULT)
        out[2 * n] += product[:, :BLOCK]
        out[2 * n + 1] += product[:, BLOCK:]


def schur_product(masked, slack, pieces, scens, part, earlier):
    steps, depth, own_width = masked.shape
    depth //= 2
    width = pieces[0].shape[1]
    rows = len(pieces) * width
    shape = (scens, rows, own_width // scens)
    return pl.pallas_call(
        schur_kernel,
        grid=(steps,),
        in_specs=[
            pl.BlockSpec((1, 2 * depth, own_width), lambda t: (t, 0, 0)),
            pl.BlockSpec(slack.shape, lambda t: (0, 0)),
            ANY,
        ]
        + [pl.BlockSpec((depth // BLOCK, width, BLOCK), lambda t: (t, 0, 0))] * len(pieces),
        out_specs=[pl.BlockSpec(shape, lambda t: (0, part, 0)), DONE_SPEC],
        out_shape=[jax.ShapeDtypeStruct((scens, 2 * rows, own_width // scens), F32), DONE],
        input_output_aliases={2: 0} if part else {},
        scratch_shapes=[pltpu.VMEM((rows, 3 * depth), BF16)],
        compiler_params=WIDE_PARAMS,
        cost_estimate=SHORT,
        name="schur",
    )(masked, slack, earlier, *pieces)


def eliminate(w):
    for first in range(0, BLOCK, SLAB):
        height = BLOCK - first
        cols = [jnp.broadcast_to(w[first:, first + k : first + k + 1], (height, BLOCK)) for k in range(SLAB)]
        left, right = w[first : first + SLAB, :BLOCK], w[first : first + SLAB, BLOCK:]
        lower, upper = [], []
        for k in range(0, SLAB, 2):
            c0, c1 = cols[k], cols[k + 1]
            a00, a10, a11 = c0[k : k + 1, :], c0[k + 1 : k + 2, :], c1[k + 1 : k + 2, :]
            inv0 = 1.0 / a00
            inv1 = a00 * (1.0 / (a00 * a11 - a10 * a10))
            ratio = a10 * inv0
            c1 = c1 - c0 * ratio
            for m in range(k + 2, SLAB):
                f0 = c0[m : m + 1, :] * inv0
                f1 = (cols[k + 1][m : m + 1, :] - c0[m : m + 1, :] * ratio) * inv1
                cols[m] = cols[m] - c0 * f0 - c1 * f1
            s0 = lax.rsqrt(a00)
            s1 = lax.rsqrt(a11 - a10 * ratio)
            low0, low1 = c0 * s0, c1 * s1
            l0, l1 = left[k : k + 1, :], left[k + 1 : k + 2, :]
            r0, r1 = right[k : k + 1, :], right[k + 1 : k + 2, :]
            l0, l1 = l0 * s0, (l1 - l0 * ratio) * s1
            r0, r1 = r0 * s0, (r1 - r0 * ratio) * s1
            if k + 2 < SLAB:
                left = left - low0[:SLAB] * l0 - low1[:SLAB] * l1
                right = right - low0[:SLAB] * r0 - low1[:SLAB] * r1
            w[first + k:first + k + 1, BLOCK:] = r0
            w[first + k + 1:first + k + 2, BLOCK:] = r1
            lower += [low0, low1]
            upper += [(l0, r0), (l1, r1)]
        if height > SLAB:
            rest0, rest1 = w[first + SLAB :, :BLOCK], w[first + SLAB :, BLOCK:]
            for k in range(SLAB):
                rest0 = rest0 - lower[k][SLAB:] * upper[k][0]
                rest1 = rest1 - lower[k][SLAB:] * upper[k][1]
            w[first + SLAB :, :BLOCK] = rest0
            w[first + SLAB :, BLOCK:] = rest1


def rows_of(place, k, width):
    return pl.ds(pl.multiple_of(place[3 + k] * width, width), width)


def solve_kernel(place, mine, other, *refs):
    *pieces, _, fwd, sol, m, w, linv = refs
    size = fwd.shape[0]
    steps = size // BLOCK
    width = pieces[0].shape[1]
    for q in range(2):
        here = pl.ds(pl.multiple_of((q + 2 * place[2]) * BLOCK, BLOCK), BLOCK)
        m[:, here] = mine[q]
        here = pl.ds(pl.multiple_of((q + 2 * (1 - place[2])) * BLOCK, BLOCK), BLOCK)
        m[:, here] = other[q]
        for k, piece in enumerate(pieces):
            m[rows_of(place, k, width), size + q * BLOCK : size + (q + 1) * BLOCK] = piece[q]
    shape = (BLOCK, BLOCK)
    eye = (lax.broadcasted_iota(jnp.int32, shape, 0) == lax.broadcasted_iota(jnp.int32, shape, 1)).astype(F32)

    for step in range(steps):
        after = (step + 1) * BLOCK
        here = slice(step * BLOCK, after)
        w[:, :BLOCK] = m[here, here]
        w[:, BLOCK:] = eye
        eliminate(w)
        inverse = w[:, BLOCK:]
        linv[step] = inverse
        m[here, after:] = dot_nn(inverse, m[here, after:])
        for later in range(step + 1, steps):
            first = later * BLOCK
            there = slice(first, first + BLOCK)
            m[there, first:] = m[there, first:] - dot_tn(m[here, there], m[here, first:])
    fwd[...] = m[:, size:]
    for step in reversed(range(steps)):
        rows = slice(step * BLOCK, (step + 1) * BLOCK)
        total = m[rows, size:]
        if step + 1 < steps:
            after = (step + 1) * BLOCK
            total = total - dot_nn(m[rows, after:size], sol[after:, :])
        sol[rows, :] = dot_tn(linv[step], total)


def directions_kernel(place, sol, mine, slack, scen_rhs, directions):
    size = sol.shape[0]
    solved = sol[...]
    own_slack = slack[:, pl.ds(pl.multiple_of(place[1] * BLOCK, BLOCK), BLOCK)]
    for s in range(2):
        moved = dot_tn(mine[:, s].reshape(size, BLOCK), solved)
        divisor = jnp.broadcast_to(own_slack[s : s + 1], (BLOCK, BLOCK)).T
        for h in range(moved.shape[1] // BLOCK):
            lanes = slice(h * BLOCK, (h + 1) * BLOCK)
            directions[s, :, lanes] = (scen_rhs[s, :, lanes] - moved[:, lanes]) / divisor


def reduced_kernel(place, schur, sol, fwd, rhs, reduced, moved_sol):
    pieces = place.shape[0] - 3
    width = sol.shape[0] // pieces
    for k in range(pieces):
        moved_sol[k * width : (k + 1) * width, :] = sol[rows_of(place, k, width), :]
    total = schur[0]
    for k in range(1, schur.shape[0]):
        total = total + schur[k]
    reduced[0] = rhs[...] - dot_tn(total, moved_sol[...])

    @pl.when(place[0] == 0)
    def _():
        reduced[0, :width] = fwd[rows_of(place, -2, width), :]


def shape_of(value):
    return jax.ShapeDtypeStruct(value.shape, value.dtype)


def with_other_core(pieces):
    return [value for piece in pieces for value in (piece, lax.ppermute(piece, "core", SWAP))]


def per_device(border, pattern, slack, first_diag, rhs, scen_rhs):
    scen_index = lax.axis_index("scen")
    core_index = lax.axis_index("core")
    pattern = jnp.transpose(pattern, (0, 2, 1))
    col_index = lax.axis_index(COL)
    cols = lax.axis_size(COL)
    scens = lax.axis_size("scen")
    chips = lax.axis_size(ALL_CHIPS)
    own, row_total, own_width = border.shape
    width = PW // cols
    nrhs = rhs.shape[1]
    blocks = row_total // BLOCK
    smem = pl.BlockSpec(memory_space=pltpu.SMEM)

    row_blocks, piece = pl.pallas_call(
        panel_kernel,
        grid=(own,),
        in_specs=[
            smem,
            pl.BlockSpec((1, row_total, BLOCK), lambda s: (s, 0, 0)),
            pl.BlockSpec((width, nrhs), lambda s: (0, 0)),
        ],
        out_specs=[
            pl.BlockSpec((blocks, 1, width, BLOCK), lambda s: (0, s, 0, 0)),
            pl.BlockSpec((own * blocks + 2, width, BLOCK), lambda s: (0, 0, 0)),
        ],
        out_shape=[
            jax.ShapeDtypeStruct((blocks, own, width, BLOCK), F32),
            jax.ShapeDtypeStruct((own * blocks + 2, width, BLOCK), F32),
        ],
        compiler_params=WIDE_PARAMS,
        name="panel",
    )(pattern, border, rhs)

    mine = lax.all_to_all(row_blocks, COL, 0, 0, tiled=True)
    along = lax.axis_size("x")
    first_way = [(2 * a + c, 2 * ((a + 1 - 2 * c) % along) + c) for a in range(along) for c in range(2)]
    second_way = [(target, source) for source, target in first_way]
    first = lax.ppermute(piece, ("x", "core"), first_way)
    second = lax.ppermute(piece, ("x", "core"), second_way)
    beside = lax.ppermute(piece, "z", SWAP)
    masked, masked_done = mask_parts(pattern, border, row_blocks)
    first = follow(masked_done, first)
    opposite = lax.ppermute(first, ("x", "core"), first_way)

    diag = jnp.where(scen_index == 0, first_diag[:width], 0.0)
    diag = lax.dynamic_update_slice_in_dim(jnp.zeros((PW,), F32), diag, col_index * width, 0).reshape(1, PW)
    x, z = lax.axis_index("x"), lax.axis_index("z")
    place = [scen_index, col_index, core_index]
    for step, side in ((0, 0), (-1, 0), (1, 0), (0, 1), (-1, 1), (1, 1), (2, 0), (2, 1)):
        for other_core in range(2):
            c = core_index if other_core == 0 else 1 - core_index
            chip_x = lax.rem(x + along + step * (1 - 2 * c), along)
            place.append((chip_x * 2 + lax.rem(z + side, 2)) * 2 + c)
    place = jnp.stack(place).astype(jnp.int32)
    half_shape = jax.ShapeDtypeStruct((2, PW, BLOCK), F32)
    kept, sent, second, beside = pl.pallas_call(
        pivot_kernel,
        in_specs=[smem, VMEM, VMEM, VMEM, ANY, ANY, ANY],
        out_specs=[VMEM, VMEM, ANY, ANY],
        out_shape=[half_shape, half_shape] + [shape_of(first)] * 2,
        scratch_shapes=[pltpu.VMEM((PW, own * BLOCK), F32)],
        input_output_aliases={5: 2, 6: 3},
        compiler_params=PARAMS,
        cost_estimate=SHORT,
        name="pivot",
    )(place, mine, slack, diag, masked_done, second, beside)

    pair = kept + lax.ppermute(sent, "core", SWAP)
    pair = lax.all_to_all(pair.reshape(chips, 2 * PW // chips, BLOCK), ALL_CHIPS, 0, 0, tiled=True)
    opposite_beside = lax.ppermute(opposite, "z", SWAP)
    first_beside = lax.ppermute(beside, ("x", "core"), first_way)
    second_beside = lax.ppermute(beside, ("x", "core"), second_way)
    near_pieces = with_other_core([piece, first, second, beside])
    schur, near_done = schur_product(masked, slack, near_pieces, scens, 0, masked_done)

    share, first_beside, second_beside, opposite_beside = pl.pallas_call(
        total_kernel,
        in_specs=[VMEM, ANY] + [ANY] * 3,
        out_specs=[VMEM] + [ANY] * 3,
        out_shape=[shape_of(v) for v in (pair, first_beside, second_beside, opposite_beside)],
        input_output_aliases={2: 1, 3: 2, 4: 3},
        compiler_params=PARAMS,
        cost_estimate=SHORT,
        name="total",
    )(pair, near_done, first_beside, second_beside, opposite_beside)
    half = lax.all_to_all(share, ALL_CHIPS, 0, 0, tiled=True).reshape(2, PW, BLOCK)
    far_pieces = with_other_core([first_beside, second_beside, opposite, opposite_beside])
    schur, far_done = schur_product(masked, slack, far_pieces, scens, 1, schur)
    half = follow(far_done, half)
    other = lax.ppermute(half, "core", SWAP)

    pieces = near_pieces + far_pieces
    fwd, sol = pl.pallas_call(
        solve_kernel,
        grid=(1,),
        in_specs=[
            smem,
            pl.BlockSpec((2, PW, BLOCK), lambda t: (0, 0, 0)),
            pl.BlockSpec((2, PW, BLOCK), lambda t: (0, 0, 0)),
        ]
        + [pl.BlockSpec((2, width, BLOCK), lambda t: (own * blocks // 2, 0, 0))] * len(pieces)
        + [ANY],
        out_specs=[pl.BlockSpec((PW, nrhs), lambda t: (0, 0))] * 2,
        out_shape=[jax.ShapeDtypeStruct((PW, nrhs), F32)] * 2,
        scratch_shapes=[
            pltpu.VMEM((PW, PW + nrhs), F32),
            pltpu.VMEM((BLOCK, 2 * BLOCK), F32),
            pltpu.VMEM((PW // BLOCK, BLOCK, BLOCK), F32),
        ],
        compiler_params=WIDE_PARAMS,
        cost_estimate=SHORT,
        name="solve",
    )(place, half, other, *pieces, far_done)
    schur = lax.all_to_all(schur, "scen", 0, 0, tiled=True)

    directions = pl.pallas_call(
        directions_kernel,
        in_specs=[smem] + [VMEM] * 4,
        out_specs=VMEM,
        out_shape=shape_of(scen_rhs),
        compiler_params=WIDE_PARAMS,
        cost_estimate=SHORT,
        name="directions",
    )(place, sol, mine, slack, scen_rhs)

    own_share = own_width // scens
    reduced = pl.pallas_call(
        reduced_kernel,
        grid_spec=pltpu.PrefetchScalarGridSpec(
            num_scalar_prefetch=1,
            grid=(1,),
            in_specs=[
                pl.BlockSpec(schur.shape, lambda t, *_: (0, 0, 0)),
                pl.BlockSpec((PW, nrhs), lambda t, *_: (0, 0)),
                pl.BlockSpec((PW, nrhs), lambda t, *_: (0, 0)),
                pl.BlockSpec((own_share, nrhs), lambda t, place, *_: (place[0], 0)),
            ],
            out_specs=pl.BlockSpec((1, own_share, nrhs), lambda t, *_: (0, 0, 0)),
            scratch_shapes=[pltpu.VMEM((PW, nrhs), F32)],
        ),
        out_shape=jax.ShapeDtypeStruct((1, own_share, nrhs), F32),
        compiler_params=PARAMS,
        cost_estimate=SHORT,
        name="reduced",
    )(place, schur, sol, fwd, rhs)
    return reduced, directions


def solution(mesh):
    scens, cols = mesh.devices.shape
    parts = Mesh(mesh.devices.reshape(scens, cols // 4, 2, 2), ("scen", "x", "z", "core"))
    return jax.shard_map(
        per_device,
        mesh=parts,
        in_specs=(
            P("scen", None, COL),
            P("scen", None, COL),
            P("scen", None),
            P(COL),
            P(COL, None),
            P("scen", COL, None),
        ),
        out_specs=(P(COL, "scen", None), P("scen", COL, None)),
        check_vma=False,
    )
```

```python
import jax
import jax.numpy as jnp
from jax import lax
from jax.experimental import pallas as pl
from jax.experimental.pallas import tpu as pltpu
from jax.sharding import Mesh, PartitionSpec as P

PW = 512
BLOCK = 128
SLAB = 8
STEPS = 8
F32 = jnp.float32
BF16 = jnp.bfloat16
COL = ("x", "z", "core")
SWAP = [(0, 1), (1, 0)]
ALL_CHIPS = ("scen", "x", "z")
DONE = jax.ShapeDtypeStruct((8, 128), F32)
DONE_SPEC = pl.BlockSpec((8, 128), lambda t: (0, 0))
ANY = pl.BlockSpec(memory_space=pl.ANY)
VMEM = pl.BlockSpec(memory_space=pltpu.VMEM)
PARAMS = pltpu.CompilerParams(vmem_limit_bytes=20 << 20)
SHORT = pl.CostEstimate(flops=1 << 20, bytes_accessed=1 << 16, transcendentals=0)
WIDE_PARAMS = pltpu.CompilerParams(vmem_limit_bytes=56 << 20)


def dot(a, b, dims, precision=lax.Precision.HIGHEST):
    return lax.dot_general(a, b, (dims, ((), ())), precision=precision, preferred_element_type=F32)


def dot_nn(a, b):
    return dot(a, b, ((1,), (0,)))


def dot_tn(a, b):
    return dot(a, b, ((0,), (0,)))


def dot_nt(a, b):
    return dot(a, b, ((1,), (1,)))


def panel_kernel(pattern, border, rhs, row_out, all_out):
    scen = pl.program_id(0)
    width = rhs.shape[0]
    blocks = row_out.shape[0]
    for i in range(blocks):
        rows = border[0, i * BLOCK : (i + 1) * BLOCK, :].T[:width]
        rows = rows * pattern[scen, 0, i].astype(F32)
        row_out[i, 0] = rows
        all_out[scen * blocks + i] = rows

    @pl.when(scen == 0)
    def _():
        for h in range(2):
            all_out[2 * blocks + h] = rhs[:, h * BLOCK : (h + 1) * BLOCK]


def pivot_kernel(place, mine, slack, diag, *refs):
    kept, sent, right = refs[3], refs[4], refs[-1]
    size = right.shape[0]
    width = mine.shape[2]
    per_block = BLOCK // width
    shift = lax.rem(place[1], per_block) * width
    lanes = lax.broadcasted_iota(jnp.int32, diag.shape, 1)
    own_lanes = (lanes >= shift) & (lanes < shift + width) & (place[0] == 0)
    own_diag = jnp.where(own_lanes, pltpu.roll(jnp.broadcast_to(diag[0:1, :], diag.shape), shift, axis=1), 0.0)[0:1]
    own_block = lax.div(place[1], per_block) * BLOCK
    for s in range(2):
        right[:, s * BLOCK : (s + 1) * BLOCK] = mine[:, s].reshape(size, BLOCK)
    own_slack = slack[:, pl.ds(pl.multiple_of(place[1] * BLOCK, BLOCK), BLOCK)]
    left = jnp.concatenate([right[:, s * BLOCK : (s + 1) * BLOCK] / own_slack[s : s + 1] for s in range(2)], axis=1)
    rows = lax.broadcasted_iota(jnp.int32, (size, BLOCK), 0)
    cols = lax.broadcasted_iota(jnp.int32, (size, BLOCK), 1)
    for out, core in ((kept, place[2]), (sent, 1 - place[2])):
        for q in range(2):
            first = pl.multiple_of((q + 2 * core) * BLOCK, BLOCK)
            piece = dot_nt(left, right[pl.ds(first, BLOCK), :])
            out[q] = piece + jnp.where((rows == cols + first) & (first == own_block), own_diag, 0.0)


def total_kernel(pair, *refs):
    shared = refs[4]
    total = pair[0]
    for k in range(1, pair.shape[0]):
        total = total + pair[k]
    for k in range(pair.shape[0]):
        shared[k] = total


def split(values):
    high = values.astype(BF16)
    return high, (values - high.astype(F32)).astype(BF16)


def mask_kernel(pattern, border, _, out, done):
    step = pl.program_id(0)
    done[...] = jnp.zeros_like(done)
    depth, width = border.shape[1:]
    per_scen = STEPS // pattern.shape[0]
    for e in range(depth // BLOCK):
        block = lax.rem(step, per_scen) * (depth // BLOCK) + e
        at = e * BLOCK
        for c in range(width // BLOCK):
            lanes = slice(c * BLOCK, (c + 1) * BLOCK)
            weight = pattern[lax.div(step, per_scen), c, block].astype(F32)
            high, low = split(border[0, at : at + BLOCK, lanes] * weight)
            out[0, at : at + BLOCK, lanes] = high
            out[0, depth + at : depth + at + BLOCK, lanes] = low


def mask_parts(pattern, border, after):
    scenarios, row_total, own_width = border.shape
    depth = scenarios * row_total // STEPS
    per_scen = row_total // depth
    return pl.pallas_call(
        mask_kernel,
        grid=(STEPS,),
        in_specs=[
            pl.BlockSpec(memory_space=pltpu.SMEM),
            pl.BlockSpec((1, depth, own_width), lambda t: (t // per_scen, t % per_scen, 0)),
            ANY,
        ],
        out_specs=[pl.BlockSpec((1, 2 * depth, own_width), lambda t: (t, 0, 0)), DONE_SPEC],
        out_shape=[jax.ShapeDtypeStruct((STEPS, 2 * depth, own_width), BF16), DONE],
        compiler_params=WIDE_PARAMS,
        cost_estimate=SHORT,
        name="mask",
    )(pattern, border, after)


def follow_kernel(*refs):
    del refs


def follow(first, value):
    return pl.pallas_call(
        follow_kernel,
        in_specs=[ANY, ANY],
        out_specs=ANY,
        out_shape=shape_of(value),
        input_output_aliases={1: 0},
        compiler_params=PARAMS,
        cost_estimate=SHORT,
        name="follow",
    )(first, value)


def schur_kernel(masked, slack, _, *refs):
    *pieces, out, done, left = refs
    step = pl.program_id(0)
    done[...] = jnp.zeros_like(done)
    count, width = pieces[0].shape[:2]
    depth = count * BLOCK
    per_scen = slack.shape[1] // depth
    for e in range(count):
        at = e * BLOCK
        first = pl.multiple_of(lax.rem(step, per_scen) * depth + at, BLOCK)
        both = slack[:, pl.ds(first, BLOCK)]
        inverse = 1.0 / jnp.where(step < per_scen, both[0:1], both[1:2])
        for k, piece in enumerate(pieces):
            high, low = split(piece[e] * inverse)
            rows = slice(k * width, (k + 1) * width)
            left[rows, at : at + BLOCK] = high
            left[rows, depth + at : depth + at + BLOCK] = high
            left[rows, 2 * depth + at : 2 * depth + at + BLOCK] = low

    @pl.when(step == 0)
    def _():
        out[...] = jnp.zeros_like(out)

    wide = 2 * BLOCK
    dims = ((1,), (0,))
    for n in range(masked.shape[2] // wide):
        lanes = slice(n * wide, (n + 1) * wide)
        product = dot(left[:, : 2 * depth], masked[0, :, lanes], dims, lax.Precision.DEFAULT)
        product += dot(left[:, 2 * depth :], masked[0, :depth, lanes], dims, lax.Precision.DEFAULT)
        out[2 * n] += product[:, :BLOCK]
        out[2 * n + 1] += product[:, BLOCK:]


def schur_product(masked, slack, pieces, scens, part, earlier):
    steps, depth, own_width = masked.shape
    depth //= 2
    width = pieces[0].shape[1]
    rows = len(pieces) * width
    shape = (scens, rows, own_width // scens)
    return pl.pallas_call(
        schur_kernel,
        grid=(steps,),
        in_specs=[
            pl.BlockSpec((1, 2 * depth, own_width), lambda t: (t, 0, 0)),
            pl.BlockSpec(slack.shape, lambda t: (0, 0)),
            ANY,
        ]
        + [pl.BlockSpec((depth // BLOCK, width, BLOCK), lambda t: (t, 0, 0))] * len(pieces),
        out_specs=[pl.BlockSpec(shape, lambda t: (0, part, 0)), DONE_SPEC],
        out_shape=[jax.ShapeDtypeStruct((scens, 2 * rows, own_width // scens), F32), DONE],
        input_output_aliases={2: 0} if part else {},
        scratch_shapes=[pltpu.VMEM((rows, 3 * depth), BF16)],
        compiler_params=WIDE_PARAMS,
        cost_estimate=SHORT,
        name="schur",
    )(masked, slack, earlier, *pieces)


def eliminate(w):
    for first in range(0, BLOCK, SLAB):
        height = BLOCK - first
        cols = [jnp.broadcast_to(w[first:, first + k : first + k + 1], (height, BLOCK)) for k in range(SLAB)]
        left, right = w[first : first + SLAB, :BLOCK], w[first : first + SLAB, BLOCK:]
        lower, upper = [], []
        for k in range(0, SLAB, 2):
            c0, c1 = cols[k], cols[k + 1]
            a00, a10, a11 = c0[k : k + 1, :], c0[k + 1 : k + 2, :], c1[k + 1 : k + 2, :]
            inv0 = 1.0 / a00
            inv1 = a00 * (1.0 / (a00 * a11 - a10 * a10))
            ratio = a10 * inv0
            c1 = c1 - c0 * ratio
            for m in range(k + 2, SLAB):
                f0 = c0[m : m + 1, :] * inv0
                f1 = (cols[k + 1][m : m + 1, :] - c0[m : m + 1, :] * ratio) * inv1
                cols[m] = cols[m] - c0 * f0 - c1 * f1
            s0 = lax.rsqrt(a00)
            s1 = lax.rsqrt(a11 - a10 * ratio)
            low0, low1 = c0 * s0, c1 * s1
            l0, l1 = left[k : k + 1, :], left[k + 1 : k + 2, :]
            r0, r1 = right[k : k + 1, :], right[k + 1 : k + 2, :]
            l0, l1 = l0 * s0, (l1 - l0 * ratio) * s1
            r0, r1 = r0 * s0, (r1 - r0 * ratio) * s1
            if k + 2 < SLAB:
                left = left - low0[:SLAB] * l0 - low1[:SLAB] * l1
                right = right - low0[:SLAB] * r0 - low1[:SLAB] * r1
            w[first + k:first + k + 1, BLOCK:] = r0
            w[first + k + 1:first + k + 2, BLOCK:] = r1
            lower += [low0, low1]
            upper += [(l0, r0), (l1, r1)]
        if height > SLAB:
            rest0, rest1 = w[first + SLAB :, :BLOCK], w[first + SLAB :, BLOCK:]
            for k in range(SLAB):
                rest0 = rest0 - lower[k][SLAB:] * upper[k][0]
                rest1 = rest1 - lower[k][SLAB:] * upper[k][1]
            w[first + SLAB :, :BLOCK] = rest0
            w[first + SLAB :, BLOCK:] = rest1


def rows_of(place, k, width):
    return pl.ds(pl.multiple_of(place[3 + k] * width, width), width)


def solve_kernel(place, mine, other, *refs):
    *pieces, _, sol, m, w, linv = refs
    size = m.shape[0]
    steps = size // BLOCK
    width = pieces[0].shape[1]
    for q in range(2):
        here = pl.ds(pl.multiple_of((q + 2 * place[2]) * BLOCK, BLOCK), BLOCK)
        m[:, here] = mine[q]
        here = pl.ds(pl.multiple_of((q + 2 * (1 - place[2])) * BLOCK, BLOCK), BLOCK)
        m[:, here] = other[q]
        for k, piece in enumerate(pieces):
            m[rows_of(place, k, width), size + q * BLOCK : size + (q + 1) * BLOCK] = piece[q]
    shape = (BLOCK, BLOCK)
    eye = (lax.broadcasted_iota(jnp.int32, shape, 0) == lax.broadcasted_iota(jnp.int32, shape, 1)).astype(F32)

    for step in range(steps):
        after = (step + 1) * BLOCK
        here = slice(step * BLOCK, after)
        w[:, :BLOCK] = m[here, here]
        w[:, BLOCK:] = eye
        eliminate(w)
        inverse = w[:, BLOCK:]
        linv[step] = inverse
        m[here, after:] = dot_nn(inverse, m[here, after:])
        for later in range(step + 1, steps):
            first = later * BLOCK
            there = slice(first, first + BLOCK)
            m[there, first:] = m[there, first:] - dot_tn(m[here, there], m[here, first:])
    sol[size:, :] = m[rows_of(place, -2, width), size:]
    for step in reversed(range(steps)):
        rows = slice(step * BLOCK, (step + 1) * BLOCK)
        total = m[rows, size:]
        if step + 1 < steps:
            after = (step + 1) * BLOCK
            total = total - dot_nn(m[rows, after:size], sol[after:size, :])
        sol[rows, :] = dot_tn(linv[step], total)


def directions_kernel(place, sol, mine, slack, scen_rhs, directions):
    size = mine.shape[0] * mine.shape[2]
    solved = sol[:size, :]
    own_slack = slack[:, pl.ds(pl.multiple_of(place[1] * BLOCK, BLOCK), BLOCK)]
    for s in range(2):
        moved = dot_tn(mine[:, s].reshape(size, BLOCK), solved)
        divisor = jnp.broadcast_to(own_slack[s : s + 1], (BLOCK, BLOCK)).T
        for h in range(moved.shape[1] // BLOCK):
            lanes = slice(h * BLOCK, (h + 1) * BLOCK)
            directions[s, :, lanes] = (scen_rhs[s, :, lanes] - moved[:, lanes]) / divisor


def reduced_kernel(place, schur, sol, rhs, reduced, moved_sol):
    pieces = place.shape[0] - 3
    width = moved_sol.shape[0] // pieces
    for k in range(pieces):
        moved_sol[k * width : (k + 1) * width, :] = sol[rows_of(place, k, width), :]
    total = schur[0]
    for k in range(1, schur.shape[0]):
        total = total + schur[k]
    reduced[0] = rhs[...] - dot_tn(total, moved_sol[...])

    @pl.when(place[0] == 0)
    def _():
        reduced[0, :width] = sol[pieces * width :, :]


def shape_of(value):
    return jax.ShapeDtypeStruct(value.shape, value.dtype)


def with_other_core(pieces):
    return [value for piece in pieces for value in (piece, lax.ppermute(piece, "core", SWAP))]


def per_device(border, pattern, slack, first_diag, rhs, scen_rhs):
    scen_index = lax.axis_index("scen")
    core_index = lax.axis_index("core")
    pattern = jnp.transpose(pattern, (0, 2, 1))
    col_index = lax.axis_index(COL)
    cols = lax.axis_size(COL)
    scens = lax.axis_size("scen")
    chips = lax.axis_size(ALL_CHIPS)
    own, row_total, own_width = border.shape
    width = PW // cols
    nrhs = rhs.shape[1]
    blocks = row_total // BLOCK
    smem = pl.BlockSpec(memory_space=pltpu.SMEM)

    row_blocks, piece = pl.pallas_call(
        panel_kernel,
        grid=(own,),
        in_specs=[
            smem,
            pl.BlockSpec((1, row_total, BLOCK), lambda s: (s, 0, 0)),
            pl.BlockSpec((width, nrhs), lambda s: (0, 0)),
        ],
        out_specs=[
            pl.BlockSpec((blocks, 1, width, BLOCK), lambda s: (0, s, 0, 0)),
            pl.BlockSpec((own * blocks + 2, width, BLOCK), lambda s: (0, 0, 0)),
        ],
        out_shape=[
            jax.ShapeDtypeStruct((blocks, own, width, BLOCK), F32),
            jax.ShapeDtypeStruct((own * blocks + 2, width, BLOCK), F32),
        ],
        compiler_params=WIDE_PARAMS,
        name="panel",
    )(pattern, border, rhs)

    mine = lax.all_to_all(row_blocks, COL, 0, 0, tiled=True)
    along = lax.axis_size("x")
    first_way = [(2 * a + c, 2 * ((a + 1 - 2 * c) % along) + c) for a in range(along) for c in range(2)]
    second_way = [(target, source) for source, target in first_way]
    first = lax.ppermute(piece, ("x", "core"), first_way)
    second = lax.ppermute(piece, ("x", "core"), second_way)
    beside = lax.ppermute(piece, "z", SWAP)
    masked, masked_done = mask_parts(pattern, border, row_blocks)
    first = follow(masked_done, first)
    opposite = lax.ppermute(first, ("x", "core"), first_way)

    diag = first_diag.reshape(-1, BLOCK)
    x, z = lax.axis_index("x"), lax.axis_index("z")
    place = [scen_index, col_index, core_index]
    for step, side in ((0, 0), (-1, 0), (1, 0), (0, 1), (-1, 1), (1, 1), (2, 0), (2, 1)):
        for other_core in range(2):
            c = core_index if other_core == 0 else 1 - core_index
            chip_x = lax.rem(x + along + step * (1 - 2 * c), along)
            place.append((chip_x * 2 + lax.rem(z + side, 2)) * 2 + c)
    place = jnp.stack(place).astype(jnp.int32)
    half_shape = jax.ShapeDtypeStruct((2, PW, BLOCK), F32)
    kept, sent, second, beside = pl.pallas_call(
        pivot_kernel,
        in_specs=[smem, VMEM, VMEM, VMEM, ANY, ANY, ANY],
        out_specs=[VMEM, VMEM, ANY, ANY],
        out_shape=[half_shape, half_shape] + [shape_of(first)] * 2,
        scratch_shapes=[pltpu.VMEM((PW, own * BLOCK), F32)],
        input_output_aliases={5: 2, 6: 3},
        compiler_params=PARAMS,
        cost_estimate=SHORT,
        name="pivot",
    )(place, mine, slack, diag, masked_done, second, beside)

    pair = kept + lax.ppermute(sent, "core", SWAP)
    pair = lax.all_to_all(pair.reshape(chips, 2 * PW // chips, BLOCK), ALL_CHIPS, 0, 0, tiled=True)
    opposite_beside = lax.ppermute(opposite, "z", SWAP)
    first_beside = lax.ppermute(beside, ("x", "core"), first_way)
    second_beside = lax.ppermute(beside, ("x", "core"), second_way)
    near_pieces = with_other_core([piece, first, second, beside])
    schur, near_done = schur_product(masked, slack, near_pieces, scens, 0, masked_done)

    share, first_beside, second_beside, opposite_beside = pl.pallas_call(
        total_kernel,
        in_specs=[VMEM, ANY] + [ANY] * 3,
        out_specs=[VMEM] + [ANY] * 3,
        out_shape=[shape_of(v) for v in (pair, first_beside, second_beside, opposite_beside)],
        input_output_aliases={2: 1, 3: 2, 4: 3},
        compiler_params=PARAMS,
        cost_estimate=SHORT,
        name="total",
    )(pair, near_done, first_beside, second_beside, opposite_beside)
    half = lax.all_to_all(share, ALL_CHIPS, 0, 0, tiled=True).reshape(2, PW, BLOCK)
    far_pieces = with_other_core([first_beside, second_beside, opposite, opposite_beside])
    schur, far_done = schur_product(masked, slack, far_pieces, scens, 1, schur)
    half = follow(far_done, half)
    other = lax.ppermute(half, "core", SWAP)

    pieces = near_pieces + far_pieces
    sol = pl.pallas_call(
        solve_kernel,
        grid=(1,),
        in_specs=[
            smem,
            pl.BlockSpec((2, PW, BLOCK), lambda t: (0, 0, 0)),
            pl.BlockSpec((2, PW, BLOCK), lambda t: (0, 0, 0)),
        ]
        + [pl.BlockSpec((2, width, BLOCK), lambda t: (own * blocks // 2, 0, 0))] * len(pieces)
        + [ANY],
        out_specs=pl.BlockSpec((PW + width, nrhs), lambda t: (0, 0)),
        out_shape=jax.ShapeDtypeStruct((PW + width, nrhs), F32),
        scratch_shapes=[
            pltpu.VMEM((PW, PW + nrhs), F32),
            pltpu.VMEM((BLOCK, 2 * BLOCK), F32),
            pltpu.VMEM((PW // BLOCK, BLOCK, BLOCK), F32),
        ],
        compiler_params=WIDE_PARAMS,
        cost_estimate=SHORT,
        name="solve",
    )(place, half, other, *pieces, far_done)
    schur = lax.all_to_all(schur, "scen", 0, 0, tiled=True)

    directions = pl.pallas_call(
        directions_kernel,
        in_specs=[smem] + [VMEM] * 4,
        out_specs=VMEM,
        out_shape=shape_of(scen_rhs),
        compiler_params=WIDE_PARAMS,
        cost_estimate=SHORT,
        name="directions",
    )(place, sol, mine, slack, scen_rhs)

    own_share = own_width // scens
    reduced = pl.pallas_call(
        reduced_kernel,
        grid_spec=pltpu.PrefetchScalarGridSpec(
            num_scalar_prefetch=1,
            grid=(1,),
            in_specs=[
                pl.BlockSpec(schur.shape, lambda t, *_: (0, 0, 0)),
                pl.BlockSpec((PW + width, nrhs), lambda t, *_: (0, 0)),
                pl.BlockSpec((own_share, nrhs), lambda t, place, *_: (place[0], 0)),
            ],
            out_specs=pl.BlockSpec((1, own_share, nrhs), lambda t, *_: (0, 0, 0)),
            scratch_shapes=[pltpu.VMEM((PW, nrhs), F32)],
        ),
        out_shape=jax.ShapeDtypeStruct((1, own_share, nrhs), F32),
        compiler_params=PARAMS,
        cost_estimate=SHORT,
        name="reduced",
    )(place, schur, sol, rhs)
    return reduced, directions


def solution(mesh):
    scens, cols = mesh.devices.shape
    parts = Mesh(mesh.devices.reshape(scens, cols // 4, 2, 2), ("scen", "x", "z", "core"))
    return jax.shard_map(
        per_device,
        mesh=parts,
        in_specs=(
            P("scen", None, COL),
            P("scen", None, COL),
            P("scen", None),
            P(COL),
            P(COL, None),
            P("scen", COL, None),
        ),
        out_specs=(P(COL, "scen", None), P("scen", COL, None)),
        check_vma=False,
    )
```
